32 devices in a mesh: pole: 2 (over y), prow: 4 (over z), pcol: 4 (over x, core).
Axes of the slice: x: 2, y: 2, z: 4, core: 2. Of those that a mesh axis runs over, the one named last changes fastest.
Arguments:
- known: float32 [8192, 4096], P(('pole', 'prow'), 'pcol'), parts along dimension 0, may hold values from -0.09375 to 0.09375
- lower_two: float32 [8192, 256], P(('pole', 'prow', 'pcol')), parts along dimension 0, may hold values from -0.5 to 0.5
- lower_one: float32 [8192, 256], P(('pole', 'prow', 'pcol')), parts along dimension 0, may hold values from -0.5 to 0.5
- top_one: float32 [512, 256], P('pole'), parts along dimension 0, may hold values from -0.375 to 0.375
- inner_two: float32 [512, 256], P('pole'), parts along dimension 0, may hold values from -6 to 6
- inner_one: float32 [512, 256], P('pole'), parts along dimension 0, may hold values from -6 to 6
- heights: int32 [16], replicated, may hold values from 128 to 256, as said below
- pattern_two: int32 [16], replicated, may hold values 0 or 1
- pattern_one: int32 [16], replicated, may hold values 0 or 1
Outputs:
- column_two: float32 [8192, 256], P(('pole', 'prow', 'pcol')), parts along dimension 0
- diag_two: float32 [512, 256], P('pole'), parts along dimension 0
- column_one: float32 [8192, 256], P(('pole', 'prow', 'pcol')), parts along dimension 0
- cross_block: float32 [512, 256], P('pole'), parts along dimension 0
- diag_one: float32 [512, 256], P('pole'), parts along dimension 0
The draws below stay inside these ranges and needn't reach their ends.
There are 2 independent parts, one for each index of `pole`. The reference program is written for one: setup_inputs(seed, part) draws one part's arguments, and reference() takes and returns one part's arrays. A program takes and returns all parts, laid end to end along the dimension named above; an argument that names none is the same for every part. Nothing has to cross between parts.
Inputs may be any that keep to these rules, and one draw needn't show every extreme that they name: `heights`: live rows of each block; some block has all 256 rows live.
All inputs are finite; a program needn't handle non-finite values.
Results may differ from the reference program's by a relative error of at most 0.000071.
Values sent between devices are 32-bit elements; how exact they have to be, the bound alone decides.
No kernel may reach another device: no remote copies, remote signals or barrier semaphores. Data moves between devices by JAX's collectives and lax.ppermute only.
A program may use at most 64 MiB of HBM per device.

```python
import jax
import jax.numpy as jnp
from jax import lax

W = 256
NB = 16
ROWS = 4096


def draw_heights(key, part):
    key = jax.random.fold_in(key, 11)
    first, second = jax.random.split(key)
    drawn = jax.random.randint(first, (NB,), W // 2, W + 1)
    full_block = jax.random.randint(second, (), 0, NB)
    return jnp.where(jnp.arange(NB) == full_block, W, drawn).astype(jnp.int32)


def with_ends(array, key, low, high):
    dims = array.shape
    index_at = [jax.random.randint(jax.random.fold_in(key, axis), (), 0, dims[axis]) for axis in range(len(dims))]
    array = array.at[tuple(index_at)].set(low)
    longest = dims.index(max(dims))
    index_at[longest] = (index_at[longest] + 1) % dims[longest]
    return array.at[tuple(index_at)].set(high)


def shard_levels(key, extent, shards, least, top_value):
    loudness, own = 1.0, jax.random.fold_in(key, 6)
    for position, shards_of in shards:
        steps = jnp.exp(jax.random.uniform(jax.random.fold_in(own, position), (shards_of,), jnp.float32, least / len(shards), top_value / len(shards)))
        loudness = loudness * jnp.repeat(steps, extent[position] // shards_of).reshape([-1 if axis == position else 1 for axis in range(len(extent))])
    return loudness


def normal_values(own_key, dims, spread, limit, shards=(), dtype=jnp.bfloat16):
    values = spread * jax.random.normal(own_key, dims, jnp.float32)
    if shards:
        values = values * shard_levels(own_key, dims, shards, -0.22, 0.18)
    return jnp.clip(values, -limit, limit).astype(dtype)


def setup_inputs(seed: int = 0, part: int = 0) -> dict:
    key_of = jax.random.split(jax.random.key(seed), 10)
    part_keys = jax.random.split(jax.random.fold_in(key_of[9], part), 10)
    known = normal_values(part_keys[0], (ROWS, ROWS), ROWS ** -0.5, 0.09375, ((0, 4), (1, 4)), jnp.float32)
    lower_two = normal_values(part_keys[1], (ROWS, W), (W // 2) ** -0.5, 0.5, ((0, 16),), jnp.float32)
    lower_one = normal_values(part_keys[2], (ROWS, W), (W // 2) ** -0.5, 0.5, ((0, 16),), jnp.float32)
    top_one = normal_values(part_keys[3], (W, W), W ** -0.5, 0.375, (), jnp.float32)
    inner_two = normal_values(part_keys[4], (W, W), 1.0, 6.0, (), jnp.float32)
    inner_one = normal_values(part_keys[5], (W, W), 1.0, 6.0, (), jnp.float32)
    heights = draw_heights(jax.random.fold_in(key_of[9], 71), part)
    pattern_two = with_ends((jax.random.randint(key_of[7], (NB,), 0, 4) < 3).astype(jnp.int32), jax.random.fold_in(key_of[7], 1), 0, 1)
    pattern_one = with_ends((jax.random.randint(key_of[8], (NB,), 0, 4) < 3).astype(jnp.int32), jax.random.fold_in(key_of[8], 1), 0, 1)
    return dict(known=known, lower_two=lower_two, lower_one=lower_one, top_one=top_one, inner_two=inner_two, inner_one=inner_one, heights=heights, pattern_two=pattern_two, pattern_one=pattern_one)


def product(left, right):
    return jnp.dot(left, right, precision=lax.Precision.HIGHEST, preferred_element_type=jnp.float32)


def reference(known, lower_two, lower_one, top_one, inner_two, inner_one, heights, pattern_two, pattern_one):
    live = (jnp.arange(W)[None, :] < heights[:, None]).astype(jnp.float32).reshape(-1)
    keep_two = live * jnp.repeat(pattern_two.astype(jnp.float32), W)
    keep_one = live * jnp.repeat(pattern_one.astype(jnp.float32), W)
    masked_two = lower_two * keep_two[:, None]
    masked_one = lower_one * keep_one[:, None]
    column_two = -(live[:, None] * product(known, masked_two))
    diag_two = inner_two - product(masked_two.T, column_two)
    column_one = -(live[:, None] * (product(known, masked_one) + product(column_two, top_one)))
    cross_block = -(product(column_two.T, masked_one) + product(diag_two, top_one))
    diag_one = inner_one - product(masked_one.T, column_one) - product(top_one.T, cross_block)
    return column_two, diag_two, column_one, cross_block, diag_one
```

```python
import functools

import jax
import jax.numpy as jnp
from jax import lax
from jax.experimental import pallas as pl
from jax.experimental.pallas import tpu as pltpu
from jax.sharding import PartitionSpec as P

F32 = jnp.float32
BF16 = jnp.bfloat16
SMEM = pl.BlockSpec(memory_space=pltpu.SMEM)
VMEM = pl.BlockSpec(memory_space=pltpu.VMEM)
ANY = pl.BlockSpec(memory_space=pl.ANY)


def product(left, right):
    return jnp.dot(left, right, precision=lax.Precision.HIGHEST, preferred_element_type=F32)


def contract(left, right):
    return lax.dot_general(
        left, right, (((0,), (0,)), ((), ())), precision=lax.Precision.HIGHEST, preferred_element_type=F32
    )


def spread_2(array, axis, root):
    mine = lax.axis_index(axis) == root
    return lax.psum(jnp.where(mine, array, jnp.zeros_like(array)), axis)


def any_mesh(
    known, lower_two, lower_one, top_one, inner_two, inner_one, heights, pattern_two, pattern_one
):
    width = top_one.shape[0]
    piece = lower_two.shape[0]
    n_col = lax.axis_size("pcol")
    ratio = lax.axis_size("prow") // n_col
    row_index = lax.axis_index("prow")
    col_index = lax.axis_index("pcol")
    live = (jnp.arange(width)[None, :] < heights[:, None]).astype(F32).reshape(-1)
    own_start = (row_index * n_col + col_index) * piece
    own_live = lax.dynamic_slice_in_dim(live, own_start, piece)

    def mask_own(lower, pattern):
        keep = live * jnp.repeat(pattern.astype(F32), width)
        return lower * lax.dynamic_slice_in_dim(keep, own_start, piece)[:, None]

    def spread(own_rows):
        band = lax.all_gather(own_rows, "pcol", axis=0, tiled=True)
        return jnp.concatenate(
            [spread_2(band, "prow", col_index * ratio + offset) for offset in range(ratio)], axis=0
        )

    def total_rows(partial_value):
        return lax.psum_scatter(partial_value, "pcol", scatter_dimension=0, tiled=True)

    own_two = mask_own(lower_two, pattern_two)
    own_one = mask_own(lower_one, pattern_one)
    partial_two = product(known, spread(own_two))
    partial_one = product(known, spread(own_one))
    column_two = -(own_live[:, None] * total_rows(partial_two))
    first_term, second_term = lax.psum(
        (contract(own_two, column_two), contract(column_two, own_one)), ("prow", "pcol")
    )
    diag_two = inner_two - first_term
    cross_block = -(second_term + product(diag_two, top_one))
    column_one = -(own_live[:, None] * (total_rows(partial_one) + product(column_two, top_one)))
    third_term = lax.psum(contract(own_one, column_one), ("prow", "pcol"))
    diag_one = inner_one - third_term - contract(top_one, cross_block)
    return (column_two, diag_two, column_one, cross_block, diag_one)


def halves(value):
    high = value.astype(BF16)
    return high, (value - high.astype(F32)).astype(BF16)


def dot3(left, right, dims):
    (lh, ll), (rh, rl) = left, right
    dot = lambda a, b: lax.dot_general(a, b, (dims, ((), ())), preferred_element_type=F32)
    return dot(lh, rh) + (dot(lh, rl) + dot(ll, rh))


ROWS_BY_COLUMNS = ((1,), (0,))
ROWS_BY_ROWS = ((0,), (0,))


def keep_rows(block, limit):
    row = lax.broadcasted_iota(jnp.int32, block.shape, 0)
    return jnp.where(row < limit, block, 0.0)


def band_kernel(n, sides, at, heights, *refs):
    patterns, refs = refs[:sides], refs[sides:]
    known = refs[0]
    gathered, plane = refs[1 : 1 + n], refs[1 + n : 1 + 2 * n]
    keep, send, sums = refs[1 + 2 * n : 4 + 2 * n]
    tiles, high, low, total, sems = refs[4 + 2 * n :]
    row, col = at[0], at[1]
    width = total.shape[-1]
    copies = [
        pltpu.make_async_copy(
            known.at[pl.ds(pl.multiple_of((a ^ col) * width, width), width)], tiles.at[a], sems.at[a]
        )
        for a in range(n)
    ]
    for copy in copies:
        copy.start()
    own = patterns[0]
    for k in range(n):
        block = row ^ k
        which = col * n + block
        h, l = halves(keep_rows(gathered[k][...], heights[which] * own[which]))
        where = pl.ds(pl.multiple_of(block * width, width), width)
        high[where] = h
        low[where] = l
    right = (high[...], low[...])
    for a in range(n):
        copies[a].wait()
        tile = dot3(halves(tiles[a]), right, ROWS_BY_COLUMNS)
        (send if a & 1 else keep)[a >> 1] = tile
        tile = halves(tile)
        which = row * n + (a ^ col)
        for s in range(sides):
            offset = plane[a].shape[0] - sides * width + s * width
            rows = plane[a][offset : offset + width]
            rows = halves(keep_rows(rows, heights[which] * patterns[s][which]))
            term = dot3(rows, tile, ROWS_BY_ROWS) if s == 0 else dot3(tile, rows, ROWS_BY_ROWS)
            total[s] = term if a == 0 else total[s] + term
    quarter = width // n
    for s in range(sides):
        for e in range(n):
            sums[e, s] = total[s, pl.ds(pl.multiple_of((e ^ col) * quarter, quarter), quarter)]


def band(at, heights, patterns, known, gathered, plane):
    n, sides = len(gathered), len(patterns)
    width = gathered[0].shape[0]
    span = known.shape[1]
    flops = 2 * 3 * (known.shape[0] * span * width + sides * known.shape[0] * width * width)
    return pl.pallas_call(
        functools.partial(band_kernel, n, sides),
        out_shape=(
            jax.ShapeDtypeStruct((n // 2, width, width), F32),
            jax.ShapeDtypeStruct((n // 2, width, width), F32),
            jax.ShapeDtypeStruct((n, sides, width // n, width), F32),
        ),
        in_specs=[SMEM] * (2 + sides) + [ANY] + [VMEM] * (2 * n),
        out_specs=(VMEM, VMEM, VMEM),
        scratch_shapes=[
            pltpu.VMEM((n, width, span), F32),
            pltpu.VMEM((span, width), BF16),
            pltpu.VMEM((span, width), BF16),
            pltpu.VMEM((sides, width, width), F32),
            pltpu.SemaphoreType.DMA((n,)),
        ],
        compiler_params=pltpu.CompilerParams(vmem_limit_bytes=40 * 2**20),
        cost_estimate=pl.CostEstimate(flops=flops, bytes_accessed=8 * 2**20, transcendentals=0),
        name="band_product",
    )(at, heights, *patterns, known, *gathered, *plane)


def blocks_kernel(n, at, top, inner_two, inner_one, *refs):
    parts, (diag_two, cross, rest, whole) = refs[:n], refs[n:]
    col = at[1]
    quarter = parts[0].shape[1]
    for e in range(n):
        for s in range(2):
            whole[s, pl.ds(pl.multiple_of((e ^ col) * quarter, quarter), quarter)] = parts[e][s]
    t = halves(top[...])
    d = inner_two[...] + whole[0]
    diag_two[...] = d
    c = whole[1] - dot3(halves(d), t, ROWS_BY_COLUMNS)
    cross[...] = c
    rest[...] = (
        inner_one[...]
        - dot3(halves(whole[1]), t, ROWS_BY_ROWS)
        - dot3(t, halves(c), ROWS_BY_ROWS)
    )


def blocks(at, top, inner_two, inner_one, parts):
    shape = jax.ShapeDtypeStruct(top.shape, F32)
    return pl.pallas_call(
        functools.partial(blocks_kernel, len(parts)),
        out_shape=(shape, shape, shape),
        in_specs=[SMEM] + [VMEM] * (3 + len(parts)),
        out_specs=(VMEM,) * 3,
        scratch_shapes=[pltpu.VMEM((2,) + top.shape, F32)],
        name="small_blocks",
    )(at, top, inner_two, inner_one, *parts)


def last_kernel(n, at, rest, *refs):
    parts, out = refs[:n], refs[n]
    col = at[1]
    quarter = parts[0].shape[1]
    for e in range(n):
        where = pl.ds(pl.multiple_of((e ^ col) * quarter, quarter), quarter)
        out[where] = rest[where] + parts[e][0]


def last(at, rest, parts):
    return pl.pallas_call(
        functools.partial(last_kernel, len(parts)),
        out_shape=jax.ShapeDtypeStruct(rest.shape, F32),
        in_specs=[SMEM] + [VMEM] * (1 + len(parts)),
        out_specs=VMEM,
        name="last_block",
    )(at, rest, *parts)


def column_kernel(at, heights, mine, other, *refs):
    n = heights.shape[0]
    limit = heights[at[0] * 4 + at[1]]
    total = mine[...] + other[...]
    if len(refs) == 1:
        refs[0][...] = keep_rows(-total, limit)
    else:
        before, top, out = refs
        total = total + dot3(halves(before[...]), halves(top[...]), ROWS_BY_COLUMNS)
        out[...] = keep_rows(-total, limit)


def column(at, heights, mine, other, *more):
    return pl.pallas_call(
        column_kernel,
        out_shape=jax.ShapeDtypeStruct(mine.shape, F32),
        in_specs=[SMEM, SMEM] + [VMEM] * (2 + len(more)),
        out_specs=VMEM,
        name="column_rows",
    )(at, heights, mine, other, *more)


def square_mesh(
    known, lower_two, lower_one, top_one, inner_two, inner_one, heights, pattern_two, pattern_one
):
    n = lax.axis_size("pcol")
    at = jnp.stack([lax.axis_index("prow"), lax.axis_index("pcol")]).astype(jnp.int32)

    def along(axis, k, array):
        return lax.ppermute(array, axis, [(i, i ^ k) for i in range(n)])

    core = functools.partial(along, "pcol", 1)
    across = functools.partial(along, "pcol", 2)

    def gather(rows):
        return [
            lax.ppermute(
                rows, ("prow", "pcol"), [(z * n + j, (j ^ k) * n + z) for z in range(n) for j in range(n)]
            )
            for k in range(n)
        ]

    def total_over_mesh(sums):
        got = core(sums[1::2])
        mine, theirs = sums[0] + got[0], sums[2] + got[1]
        mine = mine + across(theirs)
        mine = mine + along("prow", 1, mine)
        mine = mine + along("prow", 2, mine)
        other = across(mine)
        return (mine, core(mine), other, core(other))

    def total_over_row(keep, send):
        got = core(send)
        return keep[0] + got[0], across(keep[1] + got[1])

    rows_two = gather(lower_two)
    pair = jnp.concatenate([lower_two, lower_one], axis=0)
    pair_x = across(pair)
    plane = [pair, core(pair), pair_x, core(pair_x)]
    rows_one = gather(lower_one)

    keep_two, send_two, sums_two = band(
        at, heights, (pattern_two, pattern_one), known, rows_two, plane
    )
    parts_two = total_over_mesh(sums_two)
    column_two = column(at, heights, *total_over_row(keep_two, send_two))
    diag_two, cross_block, rest = blocks(at, top_one, inner_two, inner_one, parts_two)
    keep_one, send_one, sums_one = band(at, heights, (pattern_one,), known, rows_one, plane)
    parts_one = total_over_mesh(sums_one)
    column_one = column(at, heights, *total_over_row(keep_one, send_one), column_two, top_one)
    diag_one = last(at, rest, parts_one)
    return (column_two, diag_two, column_one, cross_block, diag_one)


def per_device(known, lower_two, lower_one, top_one, *rest):
    square = lax.axis_size("prow") == 4 and lax.axis_size("pcol") == 4
    body = square_mesh if square and lower_two.shape == top_one.shape else any_mesh
    return body(known, lower_two, lower_one, top_one, *rest)


def solution(mesh):
    return jax.shard_map(
        per_device,
        mesh=mesh,
        in_specs=(
            P(("pole", "prow"), "pcol"),
            P(("pole", "prow", "pcol"), None),
            P(("pole", "prow", "pcol"), None),
            P("pole", None),
            P("pole", None),
            P("pole", None),
            P(),
            P(),
            P(),
        ),
        out_specs=(
            P(("pole", "prow", "pcol"), None),
            P("pole", None),
            P(("pole", "prow", "pcol"), None),
            P("pole", None),
            P("pole", None),
        ),
        check_vma=False,
    )
```

```python
import functools

import jax
import jax.numpy as jnp
from jax import lax
from jax.experimental import pallas as pl
from jax.experimental.pallas import tpu as pltpu
from jax.sharding import PartitionSpec as P

F32 = jnp.float32
BF16 = jnp.bfloat16
HBM = pl.BlockSpec(memory_space=pltpu.HBM)
SMEM = pl.BlockSpec(memory_space=pltpu.SMEM)
VMEM = pl.BlockSpec(memory_space=pltpu.VMEM)


def product(left, right):
    return jnp.dot(left, right, precision=lax.Precision.HIGHEST, preferred_element_type=F32)


def contract(left, right):
    return lax.dot_general(
        left, right, (((0,), (0,)), ((), ())), precision=lax.Precision.HIGHEST, preferred_element_type=F32
    )


def spread_2(array, axis, root):
    mine = lax.axis_index(axis) == root
    return lax.psum(jnp.where(mine, array, jnp.zeros_like(array)), axis)


def any_mesh(
    known, lower_two, lower_one, top_one, inner_two, inner_one, heights, pattern_two, pattern_one
):
    width = top_one.shape[0]
    piece = lower_two.shape[0]
    n_col = lax.axis_size("pcol")
    ratio = lax.axis_size("prow") // n_col
    row_index = lax.axis_index("prow")
    col_index = lax.axis_index("pcol")
    live = (jnp.arange(width)[None, :] < heights[:, None]).astype(F32).reshape(-1)
    own_start = (row_index * n_col + col_index) * piece
    own_live = lax.dynamic_slice_in_dim(live, own_start, piece)

    def mask_own(lower, pattern):
        keep = live * jnp.repeat(pattern.astype(F32), width)
        return lower * lax.dynamic_slice_in_dim(keep, own_start, piece)[:, None]

    def spread(own_rows):
        band = lax.all_gather(own_rows, "pcol", axis=0, tiled=True)
        return jnp.concatenate(
            [spread_2(band, "prow", col_index * ratio + offset) for offset in range(ratio)], axis=0
        )

    def total_rows(partial_value):
        return lax.psum_scatter(partial_value, "pcol", scatter_dimension=0, tiled=True)

    own_two = mask_own(lower_two, pattern_two)
    own_one = mask_own(lower_one, pattern_one)
    partial_two = product(known, spread(own_two))
    partial_one = product(known, spread(own_one))
    column_two = -(own_live[:, None] * total_rows(partial_two))
    first_term, second_term = lax.psum(
        (contract(own_two, column_two), contract(column_two, own_one)), ("prow", "pcol")
    )
    diag_two = inner_two - first_term
    cross_block = -(second_term + product(diag_two, top_one))
    column_one = -(own_live[:, None] * (total_rows(partial_one) + product(column_two, top_one)))
    third_term = lax.psum(contract(own_one, column_one), ("prow", "pcol"))
    diag_one = inner_one - third_term - contract(top_one, cross_block)
    return (column_two, diag_two, column_one, cross_block, diag_one)


def halves(value):
    high = value.astype(BF16)
    return high, (value - high.astype(F32)).astype(BF16)


def dot3(left, right, dims):
    (lh, ll), (rh, rl) = left, right
    dot = lambda a, b: lax.dot_general(a, b, (dims, ((), ())), preferred_element_type=F32)
    return dot(lh, rh) + (dot(lh, rl) + dot(ll, rh))


ROWS_BY_COLUMNS = ((1,), (0,))
ROWS_BY_ROWS = ((0,), (0,))


def keep_rows(block, limit):
    row = lax.broadcasted_iota(jnp.int32, block.shape, 0)
    return jnp.where(row < limit, block, 0.0)


def limits(megabytes):
    return pltpu.CompilerParams(vmem_limit_bytes=megabytes * 2**20)


def cost(flops, moved):
    return pl.CostEstimate(flops=flops, bytes_accessed=moved, transcendentals=0)


def live_rows(at, n, which):
    return at[2 + which]


def kept_rows(at, n, side, which):
    return at[2 + which] * at[2 + n * n * (1 + side) + which]


def masked(block, at, n, which):
    width = block.shape[-1]
    return jnp.concatenate(
        [
            keep_rows(block[side * width : (side + 1) * width], kept_rows(at, n, side, which))
            for side in range(2)
        ],
        axis=1,
    )


def tile_copies(n, col, known, tiles, sems):
    width = tiles.shape[1]
    copies = [
        pltpu.make_async_copy(
            known.at[pl.ds(pl.multiple_of((a ^ col) * width, width), width)], tiles.at[a], sems.at[a]
        )
        for a in range(n)
    ]
    for copy in copies:
        copy.start()
    return copies


def pair_kernel(two, one, out, sems):
    rows = two.shape[0]
    copies = [
        pltpu.make_async_copy(block, out.at[pl.ds(i * rows, rows)], sems.at[i])
        for i, block in enumerate((two, one))
    ]
    for copy in copies:
        copy.start()
    for copy in copies:
        copy.wait()


def pair_up(two, one):
    rows, width = two.shape
    return pl.pallas_call(
        pair_kernel,
        out_shape=jax.ShapeDtypeStruct((2 * rows, width), F32),
        in_specs=[HBM, HBM],
        out_specs=VMEM,
        scratch_shapes=[pltpu.SemaphoreType.DMA((2,))],
        compiler_params=limits(4),
        cost_estimate=cost(0, 16 * rows * width),
        name="pair_rows",
    )(two, one)


def left_kernel(n, at, known, *refs):
    plane, (high, low, tiles, total, sems) = refs[:2], refs[2:]
    row, col = at[0], at[1]
    height = 2 * tiles.shape[1]
    copies = tile_copies(n, col, known, tiles, sems)
    for a in range(n):
        rows = plane[a >> 1][(a & 1) * height : (a & 1) * height + height]
        rows = halves(masked(rows, at, n, row * n + (a ^ col)))
        copies[a].wait()
        term = dot3(rows, halves(tiles[a]), ROWS_BY_ROWS)
        total[...] = term if a == 0 else total[...] + term
    high[...], low[...] = halves(total[...])


def left_product(n, at, known, plane):
    rows, span = known.shape
    width = rows // n
    half = jax.ShapeDtypeStruct((2 * width, span), BF16)
    return pl.pallas_call(
        functools.partial(left_kernel, n),
        out_shape=(half, half),
        in_specs=[SMEM, HBM, VMEM, VMEM],
        out_specs=(VMEM, VMEM),
        scratch_shapes=[
            pltpu.VMEM((n, width, span), F32),
            pltpu.VMEM((2 * width, span), F32),
            pltpu.SemaphoreType.DMA((n,)),
        ],
        compiler_params=limits(24),
        cost_estimate=cost(12 * rows * span * width, 4 * rows * span),
        name="left_product",
    )(at, known, *plane)


def gathered_halves(n, at, gathered, high, low):
    row, col = at[0], at[1]
    width = gathered[0].shape[-1]
    for k in range(n):
        block = row ^ k
        h, l = halves(masked(gathered[k][...], at, n, col * n + block))
        where = pl.ds(pl.multiple_of(block * width, width), width)
        high[where] = h
        low[where] = l


def sums_kernel(n, at, left_high, left_low, *refs):
    gathered, (keep, send, high, low, total) = refs[:n], refs[n:]
    col = at[1]
    width = total.shape[-1]
    gathered_halves(n, at, gathered, high, low)
    two = (high[:, :width], low[:, :width])
    one = (high[:, width:], low[:, width:])
    total[: 2 * width] = dot3((left_high[...], left_low[...]), two, ROWS_BY_COLUMNS)
    total[2 * width :] = dot3((left_high[width:], left_low[width:]), one, ROWS_BY_COLUMNS)
    quarter = width // n
    for e in range(n):
        for s in range(3):
            start = pl.multiple_of(s * width + (e ^ col) * quarter, quarter)
            where = pl.ds(((e >> 1) * 3 + s) * quarter, quarter)
            (send if e & 1 else keep)[where] = total[pl.ds(start, quarter)]


def small_sums(n, at, left, gathered):
    span = left[0].shape[1]
    width = gathered[0].shape[-1]
    half = jax.ShapeDtypeStruct((3 * width // 2, width), F32)
    return pl.pallas_call(
        functools.partial(sums_kernel, n),
        out_shape=(half, half),
        in_specs=[SMEM] + [VMEM] * (2 + n),
        out_specs=(VMEM, VMEM),
        scratch_shapes=[
            pltpu.VMEM((span, 2 * width), BF16),
            pltpu.VMEM((span, 2 * width), BF16),
            pltpu.VMEM((3 * width, width), F32),
        ],
        compiler_params=limits(16),
        cost_estimate=cost(18 * span * width * width, 4 * span * width),
        name="small_sums",
    )(at, *left, *gathered)


def band_kernel(n, at, known, *refs):
    gathered, (keep, send, tiles, high, low, sems) = refs[:n], refs[n:]
    copies = tile_copies(n, at[1], known, tiles, sems)
    gathered_halves(n, at, gathered, high, low)
    right = (high[...], low[...])
    for a in range(n):
        copies[a].wait()
        (send if a & 1 else keep)[a >> 1] = dot3(halves(tiles[a]), right, ROWS_BY_COLUMNS)


def band_product(n, at, known, gathered):
    rows, span = known.shape
    width = rows // n
    half = jax.ShapeDtypeStruct((n // 2, width, 2 * width), F32)
    return pl.pallas_call(
        functools.partial(band_kernel, n),
        out_shape=(half, half),
        in_specs=[SMEM, HBM] + [VMEM] * n,
        out_specs=(VMEM, VMEM),
        scratch_shapes=[
            pltpu.VMEM((n, width, span), F32),
            pltpu.VMEM((span, 2 * width), BF16),
            pltpu.VMEM((span, 2 * width), BF16),
            pltpu.SemaphoreType.DMA((n,)),
        ],
        compiler_params=limits(24),
        cost_estimate=cost(12 * rows * span * width, 4 * rows * span),
        name="band_product",
    )(at, known, *gathered)


def column_kernel(n, at, keep, got, other, top, two, one):
    width = top.shape[0]
    limit = live_rows(at, n, at[0] * n + at[1])
    total = keep[0] + got[0] + other[...]
    column_two = keep_rows(-total[:, :width], limit)
    two[...] = column_two
    second = total[:, width:] + dot3(halves(column_two), halves(top[...]), ROWS_BY_COLUMNS)
    one[...] = keep_rows(-second, limit)


def columns(n, at, keep, got, other, top):
    shape = jax.ShapeDtypeStruct(top.shape, F32)
    return pl.pallas_call(
        functools.partial(column_kernel, n),
        out_shape=(shape, shape),
        in_specs=[SMEM] + [VMEM] * 4,
        out_specs=(VMEM, VMEM),
        compiler_params=limits(8),
        name="column_rows",
    )(at, keep, got, other, top)


def blocks_kernel(n, at, top, inner_two, inner_one, first, second, diag_two, cross, diag_one, sums):
    col = at[1]
    quarter = top.shape[0] // n
    for e, (part, i) in enumerate(((first, 0), (second, 0), (first, 1), (second, 1))):
        for s in range(3):
            start = (i * 3 + s) * quarter
            where = pl.ds(pl.multiple_of((e ^ col) * quarter, quarter), quarter)
            sums[s, where] = part[start : start + quarter]
    t = halves(top[...])
    d = inner_two[...] + sums[0]
    diag_two[...] = d
    c = sums[1].T - dot3(halves(d), t, ROWS_BY_COLUMNS)
    cross[...] = c
    diag_one[...] = (
        inner_one[...]
        + sums[2]
        - dot3(halves(sums[1]), t, ROWS_BY_COLUMNS)
        - dot3(t, halves(c), ROWS_BY_ROWS)
    )


def small_blocks(n, at, top, inner_two, inner_one, parts):
    shape = jax.ShapeDtypeStruct(top.shape, F32)
    return pl.pallas_call(
        functools.partial(blocks_kernel, n),
        out_shape=(shape, shape, shape),
        in_specs=[SMEM] + [VMEM] * 5,
        out_specs=(VMEM,) * 3,
        scratch_shapes=[pltpu.VMEM((3,) + top.shape, F32)],
        compiler_params=limits(8),
        name="small_blocks",
    )(at, top, inner_two, inner_one, *parts)


def after(value, *others):
    return lax.optimization_barrier((value, *others))[0]


def square_mesh(
    known, lower_two, lower_one, top_one, inner_two, inner_one, heights, pattern_two, pattern_one
):
    n = lax.axis_size("pcol")
    place = jnp.stack([lax.axis_index("prow"), lax.axis_index("pcol")]).astype(jnp.int32)
    at = jnp.concatenate([place, heights, pattern_two, pattern_one])

    def along(axis, k, array):
        return lax.ppermute(array, axis, [(i, i ^ k) for i in range(n)])

    core = functools.partial(along, "pcol", 1)
    across = functools.partial(along, "pcol", 2)

    def direct(k, rows):
        pairs = [(z * n + j, (j ^ k) * n + z) for z in range(n) for j in range(n)]
        return lax.ppermute(rows, ("prow", "pcol"), pairs)

    pair = pair_up(lower_two, lower_one)
    gathered = [direct(k, pair) for k in range(n)]
    four = pair_up(pair, core(pair))
    plane = [four, across(four)]
    left = left_product(n, at, known, plane)

    keep_sums, send_sums = small_sums(n, at, left, gathered)
    mine = keep_sums + core(send_sums)
    half = mine.shape[0] // 2
    keep, send = band_product(n, after(at, mine), known, gathered)
    mine = mine[:half] + across(mine[half:])
    got = core(after(send, mine))
    mine = mine + along("prow", 1, mine)
    other = across(after(keep[1] + got[1], mine))
    mine = mine + along("prow", 2, mine)
    column_two, column_one = columns(n, at, keep, got, other, top_one)
    both = jnp.concatenate([after(mine, column_one), across(mine)])
    both = both, core(both)
    diag_two, cross_block, diag_one = small_blocks(n, at, top_one, inner_two, inner_one, both)
    return (column_two, diag_two, column_one, cross_block, diag_one)


def per_device(known, lower_two, lower_one, top_one, *rest):
    square = lax.axis_size("prow") == 4 and lax.axis_size("pcol") == 4
    body = square_mesh if square and lower_two.shape == top_one.shape else any_mesh
    return body(known, lower_two, lower_one, top_one, *rest)


def solution(mesh):
    return jax.shard_map(
        per_device,
        mesh=mesh,
        in_specs=(
            P(("pole", "prow"), "pcol"),
            P(("pole", "prow", "pcol"), None),
            P(("pole", "prow", "pcol"), None),
            P("pole", None),
            P("pole", None),
            P("pole", None),
            P(),
            P(),
            P(),
        ),
        out_specs=(
            P(("pole", "prow", "pcol"), None),
            P("pole", None),
            P(("pole", "prow", "pcol"), None),
            P("pole", None),
            P("pole", None),
        ),
        check_vma=False,
    )
```

```python
import functools

import jax
import jax.numpy as jnp
from jax import lax
from jax.experimental import pallas as pl
from jax.experimental.pallas import tpu as pltpu
from jax.sharding import PartitionSpec as P

F32 = jnp.float32
BF16 = jnp.bfloat16
HBM = pl.BlockSpec(memory_space=pltpu.HBM)
SMEM = pl.BlockSpec(memory_space=pltpu.SMEM)
VMEM = pl.BlockSpec(memory_space=pltpu.VMEM)


def product(left, right):
    return jnp.dot(left, right, precision=lax.Precision.HIGHEST, preferred_element_type=F32)


def contract(left, right):
    return lax.dot_general(
        left, right, (((0,), (0,)), ((), ())), precision=lax.Precision.HIGHEST, preferred_element_type=F32
    )


def spread_2(array, axis, root):
    mine = lax.axis_index(axis) == root
    return lax.psum(jnp.where(mine, array, jnp.zeros_like(array)), axis)


def any_mesh(
    known, lower_two, lower_one, top_one, inner_two, inner_one, heights, pattern_two, pattern_one
):
    width = top_one.shape[0]
    piece = lower_two.shape[0]
    n_col = lax.axis_size("pcol")
    ratio = lax.axis_size("prow") // n_col
    row_index = lax.axis_index("prow")
    col_index = lax.axis_index("pcol")
    live = (jnp.arange(width)[None, :] < heights[:, None]).astype(F32).reshape(-1)
    own_start = (row_index * n_col + col_index) * piece
    own_live = lax.dynamic_slice_in_dim(live, own_start, piece)

    def mask_own(lower, pattern):
        keep = live * jnp.repeat(pattern.astype(F32), width)
        return lower * lax.dynamic_slice_in_dim(keep, own_start, piece)[:, None]

    def spread(own_rows):
        band = lax.all_gather(own_rows, "pcol", axis=0, tiled=True)
        return jnp.concatenate(
            [spread_2(band, "prow", col_index * ratio + offset) for offset in range(ratio)], axis=0
        )

    def total_rows(partial_value):
        return lax.psum_scatter(partial_value, "pcol", scatter_dimension=0, tiled=True)

    own_two = mask_own(lower_two, pattern_two)
    own_one = mask_own(lower_one, pattern_one)
    partial_two = product(known, spread(own_two))
    partial_one = product(known, spread(own_one))
    column_two = -(own_live[:, None] * total_rows(partial_two))
    first_term, second_term = lax.psum(
        (contract(own_two, column_two), contract(column_two, own_one)), ("prow", "pcol")
    )
    diag_two = inner_two - first_term
    cross_block = -(second_term + product(diag_two, top_one))
    column_one = -(own_live[:, None] * (total_rows(partial_one) + product(column_two, top_one)))
    third_term = lax.psum(contract(own_one, column_one), ("prow", "pcol"))
    diag_one = inner_one - third_term - contract(top_one, cross_block)
    return (column_two, diag_two, column_one, cross_block, diag_one)


def halves(value):
    high = value.astype(BF16)
    return high, (value - high.astype(F32)).astype(BF16)


def dot3(left, right, dims):
    (lh, ll), (rh, rl) = left, right
    dot = lambda a, b: lax.dot_general(a, b, (dims, ((), ())), preferred_element_type=F32)
    return dot(lh, rh) + (dot(lh, rl) + dot(ll, rh))


ROWS_BY_COLUMNS = ((1,), (0,))
ROWS_BY_ROWS = ((0,), (0,))


def keep_rows(block, limit):
    row = lax.broadcasted_iota(jnp.int32, block.shape, 0)
    return jnp.where(row < limit, block, 0.0)


def limits(megabytes):
    return pltpu.CompilerParams(vmem_limit_bytes=megabytes * 2**20)


def cost(flops, moved):
    return pl.CostEstimate(flops=flops, bytes_accessed=moved, transcendentals=0)


def live_rows(at, n, which):
    return at[2 + which]


def kept_rows(at, n, side, which):
    return at[2 + which] * at[2 + n * n * (1 + side) + which]


def masked(block, at, n, which):
    width = block.shape[-1]
    return jnp.concatenate(
        [
            keep_rows(block[side * width : (side + 1) * width], kept_rows(at, n, side, which))
            for side in range(2)
        ],
        axis=1,
    )


def tile_rows(a, col, width):
    return pl.ds(pl.multiple_of((a ^ col) * width, width), width)


def stack_kernel(*refs):
    blocks, out, sems = refs[:-2], refs[-2], refs[-1]
    copies, start = [], 0
    for i, block in enumerate(blocks):
        rows = block.shape[0]
        copies.append(pltpu.make_async_copy(block, out.at[pl.ds(start, rows)], sems.at[i]))
        start += rows
    for copy in copies:
        copy.start()
    for copy in copies:
        copy.wait()


def stack(*blocks):
    rows = sum(block.shape[0] for block in blocks)
    width = blocks[0].shape[1]
    return pl.pallas_call(
        stack_kernel,
        out_shape=jax.ShapeDtypeStruct((rows, width), F32),
        in_specs=[HBM] * len(blocks),
        out_specs=VMEM,
        scratch_shapes=[pltpu.SemaphoreType.DMA((len(blocks),))],
        compiler_params=limits(4),
        cost_estimate=cost(0, 8 * rows * width),
        name="stack_rows",
    )(*blocks)


def left_terms(n, first, at, known, plane):
    row, col = at[0], at[1]
    width = known.shape[0] // n
    terms = []
    for i in range(2):
        rows = plane[2 * i * width : 2 * (i + 1) * width]
        rows = halves(masked(rows, at, n, row * n + ((first + i) ^ col)))
        terms.append(dot3(rows, halves(known[tile_rows(first + i, col, width)]), ROWS_BY_ROWS))
    return terms[0] + terms[1]


def left_first_kernel(n, at, known, plane, out):
    out[...] = left_terms(n, 0, at, known, plane)


def left_last_kernel(n, at, known, plane, before, high, low):
    total = before[...] + left_terms(n, 2, at, known, plane)
    high[...], low[...] = halves(total)


def call(kernel, name, megabytes, estimate, out_shape, *arrays, scratch=()):
    return pl.pallas_call(
        kernel,
        out_shape=out_shape,
        in_specs=[SMEM] + [VMEM] * (len(arrays) - 1),
        out_specs=jax.tree.map(lambda _: VMEM, out_shape),
        scratch_shapes=scratch,
        compiler_params=limits(megabytes),
        cost_estimate=estimate,
        name=name,
    )(*arrays)


def left_product(n, at, known, here, there):
    rows, span = known.shape
    shape = (2 * rows // n, span)
    half = jax.ShapeDtypeStruct(shape, BF16)
    first = call(
        functools.partial(left_first_kernel, n), "left_first", 14, cost(0, 0),
        jax.ShapeDtypeStruct(shape, F32), at, known, here,
    )
    return call(
        functools.partial(left_last_kernel, n), "left_last", 14, cost(0, 0),
        (half, half), at, known, there, first,
    )


def arrived_columns(row, m, width):
    return pl.ds(pl.multiple_of(((row >> 1) ^ m) * (2 * width), 2 * width), 2 * width)


def sums_kernel(n, m, at, left_high, left_low, arrived, *refs):
    before, refs = (None, refs) if m == 0 else (refs[0], refs[1:])
    out, high, low = refs[:-2], refs[-2], refs[-1]
    row, col = at[0], at[1]
    width = arrived.shape[-1]
    for e in range(2):
        block = row ^ (2 * m + e)
        rows = arrived[2 * e * width : 2 * (e + 1) * width]
        where = pl.ds(pl.multiple_of((block & 1) * width, width), width)
        high[where], low[where] = halves(masked(rows, at, n, col * n + block))
    columns = arrived_columns(row, m, width)
    left = (left_high[:, columns], left_low[:, columns])
    two = (high[:, :width], low[:, :width])
    one = (high[:, width:], low[:, width:])
    first = dot3(left, two, ROWS_BY_COLUMNS)
    second = dot3((left[0][width:], left[1][width:]), one, ROWS_BY_COLUMNS)
    if m == 0:
        out[0][: 2 * width] = first
        out[0][2 * width :] = second
        return
    keep, send, total = out
    total[: 2 * width] = before[: 2 * width] + first
    total[2 * width :] = before[2 * width :] + second
    quarter = width // n
    for e in range(n):
        for s in range(3):
            start = pl.multiple_of(s * width + (e ^ col) * quarter, quarter)
            where = pl.ds(((e >> 1) * 3 + s) * quarter, quarter)
            (send if e & 1 else keep)[where] = total[pl.ds(start, quarter)]


def small_sums(n, at, left, arrived):
    width = arrived[0].shape[-1]
    part = jax.ShapeDtypeStruct((2 * width, 2 * width), BF16)
    whole = jax.ShapeDtypeStruct((3 * width, width), F32)
    half = jax.ShapeDtypeStruct((3 * width // 2, width), F32)
    estimate = cost(18 * 2 * width * width * width, 0)
    total, *first = call(
        functools.partial(sums_kernel, n, 0), "first_sums", 8, estimate,
        (whole, part, part), at, *left, arrived[0],
    )
    keep, send, _, *second = call(
        functools.partial(sums_kernel, n, 1), "last_sums", 8, estimate,
        (half, half, whole, part, part), at, *left, arrived[1], total,
    )
    return keep, send, (*first, *second)


def band_kernel(n, first, at, known, *refs):
    right, out = refs[:4], refs[4]
    row, col = at[0], at[1]
    width = right[0].shape[0] // 2
    for i in range(n // 2):
        tile = tile_rows(first + 2 * i, col, width)
        terms = [
            dot3(
                halves(known[tile, arrived_columns(row, m, width)]),
                (right[2 * m][...], right[2 * m + 1][...]),
                ROWS_BY_COLUMNS,
            )
            for m in range(2)
        ]
        out[i] = terms[0] + terms[1]


def band_product(n, first, at, known, right):
    rows, span = known.shape
    width = rows // n
    return call(
        functools.partial(band_kernel, n, first), "band_product", 14,
        cost(6 * rows * span * width, 2 * rows * span),
        jax.ShapeDtypeStruct((n // 2, width, 2 * width), F32), at, known, *right,
    )


def column_kernel(n, at, keep, got, other, top, two, one):
    width = top.shape[0]
    limit = live_rows(at, n, at[0] * n + at[1])
    total = keep[0] + got[0] + other[...]
    column_two = keep_rows(-total[:, :width], limit)
    two[...] = column_two
    second = total[:, width:] + dot3(halves(column_two), halves(top[...]), ROWS_BY_COLUMNS)
    one[...] = keep_rows(-second, limit)


def columns(n, at, keep, got, other, top):
    shape = jax.ShapeDtypeStruct(top.shape, F32)
    return pl.pallas_call(
        functools.partial(column_kernel, n),
        out_shape=(shape, shape),
        in_specs=[SMEM] + [VMEM] * 4,
        out_specs=(VMEM, VMEM),
        compiler_params=limits(8),
        name="column_rows",
    )(at, keep, got, other, top)


def blocks_kernel(n, at, top, inner_two, inner_one, first, second, diag_two, cross, diag_one, sums):
    col = at[1]
    quarter = top.shape[0] // n
    for e, (part, i) in enumerate(((first, 0), (second, 0), (first, 1), (second, 1))):
        for s in range(3):
            start = (i * 3 + s) * quarter
            where = pl.ds(pl.multiple_of((e ^ col) * quarter, quarter), quarter)
            sums[s, where] = part[start : start + quarter]
    t = halves(top[...])
    d = inner_two[...] + sums[0]
    diag_two[...] = d
    c = sums[1].T - dot3(halves(d), t, ROWS_BY_COLUMNS)
    cross[...] = c
    diag_one[...] = (
        inner_one[...]
        + sums[2]
        - dot3(halves(sums[1]), t, ROWS_BY_COLUMNS)
        - dot3(t, halves(c), ROWS_BY_ROWS)
    )


def small_blocks(n, at, top, inner_two, inner_one, parts):
    shape = jax.ShapeDtypeStruct(top.shape, F32)
    return pl.pallas_call(
        functools.partial(blocks_kernel, n),
        out_shape=(shape, shape, shape),
        in_specs=[SMEM] + [VMEM] * 5,
        out_specs=(VMEM,) * 3,
        scratch_shapes=[pltpu.VMEM((3,) + top.shape, F32)],
        compiler_params=limits(8),
        name="small_blocks",
    )(at, top, inner_two, inner_one, *parts)


def after(value, *others):
    return lax.optimization_barrier((value, *others))[0]


def square_mesh(
    known, lower_two, lower_one, top_one, inner_two, inner_one, heights, pattern_two, pattern_one
):
    n = lax.axis_size("pcol")
    width = top_one.shape[0]
    place = jnp.stack([lax.axis_index("prow"), lax.axis_index("pcol")]).astype(jnp.int32)
    at = jnp.concatenate([place, heights, pattern_two, pattern_one])

    def along(axis, k, array):
        return lax.ppermute(array, axis, [(i, i ^ k) for i in range(n)])

    core = functools.partial(along, "pcol", 1)
    across = functools.partial(along, "pcol", 2)

    def direct(k, rows):
        pairs = [(z * n + j, (j ^ k) * n + z) for z in range(n) for j in range(n)]
        return lax.ppermute(rows, ("prow", "pcol"), pairs)

    four = stack(stack(lower_two, lower_one), core(lower_two), core(lower_one))
    gathered = [direct(k, four) for k in range(0, n, 2)]
    other = [across(lower_two), across(lower_one)]
    there = stack(*other, *[core(rows) for rows in other])
    left = left_product(n, at, known, four, there)

    keep_sums, send_sums, right = small_sums(n, at, left, gathered)
    mine = keep_sums + core(send_sums)
    half = mine.shape[0] // 2
    send = band_product(n, 1, after(at, mine), known, right)
    mine = mine[:half] + across(mine[half:])
    got = core(after(send, mine))
    keep = band_product(n, 0, after(at, mine, send), known, right)
    mine = mine + along("prow", 1, mine)
    other = across(after(keep[1] + got[1], mine))
    mine = mine + along("prow", 2, mine)
    column_two, column_one = columns(n, at, keep, got, other, top_one)
    both = jnp.concatenate([after(mine, column_one), across(mine)])
    both = both, core(both)
    diag_two, cross_block, diag_one = small_blocks(n, at, top_one, inner_two, inner_one, both)
    return (column_two, diag_two, column_one, cross_block, diag_one)


def per_device(known, lower_two, lower_one, top_one, *rest):
    square = lax.axis_size("prow") == 4 and lax.axis_size("pcol") == 4
    body = square_mesh if square and lower_two.shape == top_one.shape else any_mesh
    return body(known, lower_two, lower_one, top_one, *rest)


def solution(mesh):
    return jax.shard_map(
        per_device,
        mesh=mesh,
        in_specs=(
            P(("pole", "prow"), "pcol"),
            P(("pole", "prow", "pcol"), None),
            P(("pole", "prow", "pcol"), None),
            P("pole", None),
            P("pole", None),
            P("pole", None),
            P(),
            P(),
            P(),
        ),
        out_specs=(
            P(("pole", "prow", "pcol"), None),
            P("pole", None),
            P(("pole", "prow", "pcol"), None),
            P("pole", None),
            P("pole", None),
        ),
        check_vma=False,
    )
```

```python
import functools

import jax
import jax.numpy as jnp
from jax import lax
from jax.experimental import pallas as pl
from jax.experimental.pallas import tpu as pltpu
from jax.sharding import PartitionSpec as P

F32 = jnp.float32
BF16 = jnp.bfloat16
HBM = pl.BlockSpec(memory_space=pltpu.HBM)
SMEM = pl.BlockSpec(memory_space=pltpu.SMEM)
VMEM = pl.BlockSpec(memory_space=pltpu.VMEM)


def product(left, right):
    return jnp.dot(left, right, precision=lax.Precision.HIGHEST, preferred_element_type=F32)


def contract(left, right):
    return lax.dot_general(
        left, right, (((0,), (0,)), ((), ())), precision=lax.Precision.HIGHEST, preferred_element_type=F32
    )


def spread_2(array, axis, root):
    mine = lax.axis_index(axis) == root
    return lax.psum(jnp.where(mine, array, jnp.zeros_like(array)), axis)


def any_mesh(
    known, lower_two, lower_one, top_one, inner_two, inner_one, heights, pattern_two, pattern_one
):
    width = top_one.shape[0]
    piece = lower_two.shape[0]
    n_col = lax.axis_size("pcol")
    ratio = lax.axis_size("prow") // n_col
    row_index = lax.axis_index("prow")
    col_index = lax.axis_index("pcol")
    live = (jnp.arange(width)[None, :] < heights[:, None]).astype(F32).reshape(-1)
    own_start = (row_index * n_col + col_index) * piece
    own_live = lax.dynamic_slice_in_dim(live, own_start, piece)

    def mask_own(lower, pattern):
        keep = live * jnp.repeat(pattern.astype(F32), width)
        return lower * lax.dynamic_slice_in_dim(keep, own_start, piece)[:, None]

    def spread(own_rows):
        band = lax.all_gather(own_rows, "pcol", axis=0, tiled=True)
        return jnp.concatenate(
            [spread_2(band, "prow", col_index * ratio + offset) for offset in range(ratio)], axis=0
        )

    def total_rows(partial_value):
        return lax.psum_scatter(partial_value, "pcol", scatter_dimension=0, tiled=True)

    own_two = mask_own(lower_two, pattern_two)
    own_one = mask_own(lower_one, pattern_one)
    partial_two = product(known, spread(own_two))
    partial_one = product(known, spread(own_one))
    column_two = -(own_live[:, None] * total_rows(partial_two))
    first_term, second_term = lax.psum(
        (contract(own_two, column_two), contract(column_two, own_one)), ("prow", "pcol")
    )
    diag_two = inner_two - first_term
    cross_block = -(second_term + product(diag_two, top_one))
    column_one = -(own_live[:, None] * (total_rows(partial_one) + product(column_two, top_one)))
    third_term = lax.psum(contract(own_one, column_one), ("prow", "pcol"))
    diag_one = inner_one - third_term - contract(top_one, cross_block)
    return (column_two, diag_two, column_one, cross_block, diag_one)


def halves(value):
    high = value.astype(BF16)
    return high, (value - high.astype(F32)).astype(BF16)


def dot3(left, right, dims):
    (lh, ll), (rh, rl) = left, right
    dot = lambda a, b: lax.dot_general(a, b, (dims, ((), ())), preferred_element_type=F32)
    return dot(lh, rh) + (dot(lh, rl) + dot(ll, rh))


ROWS_BY_COLUMNS = ((1,), (0,))
ROWS_BY_ROWS = ((0,), (0,))


def keep_rows(block, limit):
    row = lax.broadcasted_iota(jnp.int32, block.shape, 0)
    return jnp.where(row < limit, block, 0.0)


def limits(megabytes):
    return pltpu.CompilerParams(vmem_limit_bytes=megabytes * 2**20)


def cost(flops, moved):
    return pl.CostEstimate(flops=flops, bytes_accessed=moved, transcendentals=0)


def live_rows(at, n, which):
    return at[2 + which]


def kept_rows(at, n, side, which):
    return at[2 + which] * at[2 + n * n * (1 + side) + which]


def masked(block, at, n, which):
    width = block.shape[-1]
    return jnp.concatenate(
        [
            keep_rows(block[side * width : (side + 1) * width], kept_rows(at, n, side, which))
            for side in range(2)
        ],
        axis=1,
    )


def tile_rows(a, col, width):
    return pl.ds(pl.multiple_of((a ^ col) * width, width), width)


def stack_kernel(*refs):
    blocks, out, sems = refs[:-2], refs[-2], refs[-1]
    copies, start = [], 0
    for i, block in enumerate(blocks):
        rows = block.shape[0]
        copies.append(pltpu.make_async_copy(block, out.at[pl.ds(start, rows)], sems.at[i]))
        start += rows
    for copy in copies:
        copy.start()
    for copy in copies:
        copy.wait()


def stack(*blocks):
    rows = sum(block.shape[0] for block in blocks)
    width = blocks[0].shape[1]
    return pl.pallas_call(
        stack_kernel,
        out_shape=jax.ShapeDtypeStruct((rows, width), F32),
        in_specs=[HBM] * len(blocks),
        out_specs=VMEM,
        scratch_shapes=[pltpu.SemaphoreType.DMA((len(blocks),))],
        compiler_params=limits(4),
        cost_estimate=cost(0, 8 * rows * width),
        name="stack_rows",
    )(*blocks)


def left_term(n, a, at, known, two, one):
    row, col = at[0], at[1]
    rows = jnp.concatenate([two, one], axis=0)
    rows = halves(masked(rows, at, n, row * n + (a ^ col)))
    tile = known[tile_rows(a, col, two.shape[0])]
    return dot3(rows, halves(tile), ROWS_BY_ROWS)


def left_first_kernel(n, at, known, here, out):
    blocks = here[...].reshape(4, -1, here.shape[1])
    out[...] = left_term(n, 0, at, known, blocks[0], blocks[1])
    out[...] += left_term(n, 1, at, known, blocks[2], blocks[3])


def left_last_kernel(n, at, known, two, one, core_two, core_one, before, high, low):
    total = before[...] + left_term(n, 2, at, known, two[...], one[...])
    total = total + left_term(n, 3, at, known, core_two[...], core_one[...])
    high[...], low[...] = halves(total)


def call(kernel, name, megabytes, estimate, out_shape, *arrays, scratch=()):
    return pl.pallas_call(
        kernel,
        out_shape=out_shape,
        in_specs=[SMEM] + [VMEM] * (len(arrays) - 1),
        out_specs=jax.tree.map(lambda _: VMEM, out_shape),
        scratch_shapes=scratch,
        compiler_params=limits(megabytes),
        cost_estimate=estimate,
        name=name,
    )(*arrays)


def left_first(n, at, known, here):
    rows, span = known.shape
    shape = jax.ShapeDtypeStruct((2 * rows // n, span), F32)
    kernel = functools.partial(left_first_kernel, n)
    return call(kernel, "left_first", 14, cost(0, 0), shape, at, known, here)


def left_last(n, at, known, there, first):
    half = jax.ShapeDtypeStruct(first.shape, BF16)
    kernel = functools.partial(left_last_kernel, n)
    return call(kernel, "left_last", 14, cost(0, 0), (half, half), at, known, *there, first)


FIRST_ARRIVAL = 1


def arrived_columns(row, m, width):
    return pl.ds(pl.multiple_of(((row >> 1) ^ m) * (2 * width), 2 * width), 2 * width)


def sums_kernel(n, m, at, left_high, left_low, arrived, *refs):
    row, col = at[0], at[1]
    width = arrived.shape[-1]
    high, low = refs[-2:] if len(refs) == 3 else refs[3:5]
    for e in range(2):
        block = row ^ (2 * m + e)
        rows = arrived[2 * e * width : 2 * (e + 1) * width]
        where = pl.ds(pl.multiple_of((block & 1) * width, width), width)
        high[where], low[where] = halves(masked(rows, at, n, col * n + block))
    columns = arrived_columns(row, m, width)
    left = (left_high[:, columns], left_low[:, columns])
    two = (high[:, :width], low[:, :width])
    one = (high[:, width:], low[:, width:])
    first = dot3(left, two, ROWS_BY_COLUMNS)
    second = dot3((left[0][width:], left[1][width:]), one, ROWS_BY_COLUMNS)
    if len(refs) == 3:
        out = refs[0]
        out[: 2 * width] = first
        out[2 * width :] = second
        return
    before, keep, send, total = refs[0], refs[1], refs[2], refs[5]
    total[: 2 * width] = before[: 2 * width] + first
    total[2 * width :] = before[2 * width :] + second
    quarter = width // n
    for e in range(n):
        for s in range(3):
            start = pl.multiple_of(s * width + (e ^ col) * quarter, quarter)
            where = pl.ds(((e >> 1) * 3 + s) * quarter, quarter)
            (send if e & 1 else keep)[where] = total[pl.ds(start, quarter)]


def small_sums(n, at, left, arrived):
    width = arrived[0].shape[-1]
    part = jax.ShapeDtypeStruct((2 * width, 2 * width), BF16)
    whole = jax.ShapeDtypeStruct((3 * width, width), F32)
    half = jax.ShapeDtypeStruct((3 * width // 2, width), F32)
    estimate = cost(18 * 2 * width * width * width, 0)
    total, *first = call(
        functools.partial(sums_kernel, n, FIRST_ARRIVAL), "first_sums", 8, estimate,
        (whole, part, part), at, *left, arrived[FIRST_ARRIVAL],
    )
    keep, send, *last = call(
        functools.partial(sums_kernel, n, 1 - FIRST_ARRIVAL), "last_sums", 8, estimate,
        (half, half, part, part), at, *left, arrived[1 - FIRST_ARRIVAL], total,
        scratch=[pltpu.VMEM((3 * width, width), F32)],
    )
    return keep, send, (*first, *last) if FIRST_ARRIVAL == 0 else (*last, *first)


def band_kernel(n, first, at, known, *refs):
    right, out = refs[:4], refs[4]
    row, col = at[0], at[1]
    width = right[0].shape[0] // 2
    for i in range(n // 2):
        tile = tile_rows(first + 2 * i, col, width)
        terms = [
            dot3(
                halves(known[tile, arrived_columns(row, m, width)]),
                (right[2 * m][...], right[2 * m + 1][...]),
                ROWS_BY_COLUMNS,
            )
            for m in range(2)
        ]
        out[i] = terms[0] + terms[1]


def band_product(n, first, at, known, right):
    rows, span = known.shape
    width = rows // n
    return call(
        functools.partial(band_kernel, n, first), "band_product", 14,
        cost(6 * rows * span * width, 2 * rows * span),
        jax.ShapeDtypeStruct((n // 2, width, 2 * width), F32), at, known, *right,
    )


def column_kernel(n, at, keep, got, other, top, two, one):
    width = top.shape[0]
    limit = live_rows(at, n, at[0] * n + at[1])
    total = keep[0] + got[0] + other[...]
    column_two = keep_rows(-total[:, :width], limit)
    two[...] = column_two
    second = total[:, width:] + dot3(halves(column_two), halves(top[...]), ROWS_BY_COLUMNS)
    one[...] = keep_rows(-second, limit)


def columns(n, at, keep, got, other, top):
    shape = jax.ShapeDtypeStruct(top.shape, F32)
    return pl.pallas_call(
        functools.partial(column_kernel, n),
        out_shape=(shape, shape),
        in_specs=[SMEM] + [VMEM] * 4,
        out_specs=(VMEM, VMEM),
        compiler_params=limits(8),
        name="column_rows",
    )(at, keep, got, other, top)


def blocks_kernel(n, at, top, inner_two, inner_one, first, second, diag_two, cross, diag_one, sums):
    col = at[1]
    quarter = top.shape[0] // n
    for e, (part, i) in enumerate(((first, 0), (second, 0), (first, 1), (second, 1))):
        for s in range(3):
            start = (i * 3 + s) * quarter
            where = pl.ds(pl.multiple_of((e ^ col) * quarter, quarter), quarter)
            sums[s, where] = part[start : start + quarter]
    t = halves(top[...])
    d = inner_two[...] + sums[0]
    diag_two[...] = d
    c = sums[1].T - dot3(halves(d), t, ROWS_BY_COLUMNS)
    cross[...] = c
    diag_one[...] = (
        inner_one[...]
        + sums[2]
        - dot3(halves(sums[1]), t, ROWS_BY_COLUMNS)
        - dot3(t, halves(c), ROWS_BY_ROWS)
    )


def small_blocks(n, at, top, inner_two, inner_one, parts):
    shape = jax.ShapeDtypeStruct(top.shape, F32)
    return pl.pallas_call(
        functools.partial(blocks_kernel, n),
        out_shape=(shape, shape, shape),
        in_specs=[SMEM] + [VMEM] * 5,
        out_specs=(VMEM,) * 3,
        scratch_shapes=[pltpu.VMEM((3,) + top.shape, F32)],
        compiler_params=limits(8),
        name="small_blocks",
    )(at, top, inner_two, inner_one, *parts)


def after(value, *others):
    return lax.optimization_barrier((value, *others))[0]


def square_mesh(
    known, lower_two, lower_one, top_one, inner_two, inner_one, heights, pattern_two, pattern_one
):
    n = lax.axis_size("pcol")
    width = top_one.shape[0]
    place = jnp.stack([lax.axis_index("prow"), lax.axis_index("pcol")]).astype(jnp.int32)
    at = jnp.concatenate([place, heights, pattern_two, pattern_one])

    def along(axis, k, array):
        return lax.ppermute(array, axis, [(i, i ^ k) for i in range(n)])

    core = functools.partial(along, "pcol", 1)
    across = functools.partial(along, "pcol", 2)

    def direct(k, rows):
        pairs = [(z * n + j, (j ^ k) * n + z) for z in range(n) for j in range(n)]
        return lax.ppermute(rows, ("prow", "pcol"), pairs)

    four = stack(stack(lower_two, lower_one), core(lower_two), core(lower_one))
    gathered = [direct(k, four) for k in range(0, n, 2)]
    first = left_first(n, at, known, four)
    there = [across(lower_two), across(lower_one)]
    there += [core(after(rows, first)) for rows in there]
    left = left_last(n, at, known, there, first)

    keep_sums, send_sums, right = small_sums(n, at, left, gathered)
    mine = keep_sums + core(send_sums)
    half = mine.shape[0] // 2
    send = band_product(n, 1, after(at, mine), known, right)
    mine = mine[:half] + across(mine[half:])
    got = core(after(send, mine))
    keep = band_product(n, 0, after(at, mine, send), known, right)
    mine = mine + along("prow", 1, mine)
    other = across(after(keep[1] + got[1], mine))
    mine = mine + along("prow", 2, mine)
    column_two, column_one = columns(n, at, keep, got, other, top_one)
    both = jnp.concatenate([after(mine, column_one), across(mine)])
    both = both, core(both)
    diag_two, cross_block, diag_one = small_blocks(n, at, top_one, inner_two, inner_one, both)
    return (column_two, diag_two, column_one, cross_block, diag_one)


def per_device(known, lower_two, lower_one, top_one, *rest):
    square = lax.axis_size("prow") == 4 and lax.axis_size("pcol") == 4
    body = square_mesh if square and lower_two.shape == top_one.shape else any_mesh
    return body(known, lower_two, lower_one, top_one, *rest)


def solution(mesh):
    return jax.shard_map(
        per_device,
        mesh=mesh,
        in_specs=(
            P(("pole", "prow"), "pcol"),
            P(("pole", "prow", "pcol"), None),
            P(("pole", "prow", "pcol"), None),
            P("pole", None),
            P("pole", None),
            P("pole", None),
            P(),
            P(),
            P(),
        ),
        out_specs=(
            P(("pole", "prow", "pcol"), None),
            P("pole", None),
            P(("pole", "prow", "pcol"), None),
            P("pole", None),
            P("pole", None),
        ),
        check_vma=False,
    )
```

```python
import functools

import jax
import jax.numpy as jnp
from jax import lax
from jax.experimental import pallas as pl
from jax.experimental.pallas import tpu as pltpu
from jax.sharding import PartitionSpec as P

F32 = jnp.float32
BF16 = jnp.bfloat16
HBM = pl.BlockSpec(memory_space=pltpu.HBM)
SMEM = pl.BlockSpec(memory_space=pltpu.SMEM)
VMEM = pl.BlockSpec(memory_space=pltpu.VMEM)


def product(left, right):
    return jnp.dot(left, right, precision=lax.Precision.HIGHEST, preferred_element_type=F32)


def contract(left, right):
    return lax.dot_general(
        left, right, (((0,), (0,)), ((), ())), precision=lax.Precision.HIGHEST, preferred_element_type=F32
    )


def spread_2(array, axis, root):
    mine = lax.axis_index(axis) == root
    return lax.psum(jnp.where(mine, array, jnp.zeros_like(array)), axis)


def any_mesh(
    known, lower_two, lower_one, top_one, inner_two, inner_one, heights, pattern_two, pattern_one
):
    width = top_one.shape[0]
    piece = lower_two.shape[0]
    n_col = lax.axis_size("pcol")
    ratio = lax.axis_size("prow") // n_col
    row_index = lax.axis_index("prow")
    col_index = lax.axis_index("pcol")
    live = (jnp.arange(width)[None, :] < heights[:, None]).astype(F32).reshape(-1)
    own_start = (row_index * n_col + col_index) * piece
    own_live = lax.dynamic_slice_in_dim(live, own_start, piece)

    def mask_own(lower, pattern):
        keep = live * jnp.repeat(pattern.astype(F32), width)
        return lower * lax.dynamic_slice_in_dim(keep, own_start, piece)[:, None]

    def spread(own_rows):
        band = lax.all_gather(own_rows, "pcol", axis=0, tiled=True)
        return jnp.concatenate(
            [spread_2(band, "prow", col_index * ratio + offset) for offset in range(ratio)], axis=0
        )

    def total_rows(partial_value):
        return lax.psum_scatter(partial_value, "pcol", scatter_dimension=0, tiled=True)

    own_two = mask_own(lower_two, pattern_two)
    own_one = mask_own(lower_one, pattern_one)
    partial_two = product(known, spread(own_two))
    partial_one = product(known, spread(own_one))
    column_two = -(own_live[:, None] * total_rows(partial_two))
    first_term, second_term = lax.psum(
        (contract(own_two, column_two), contract(column_two, own_one)), ("prow", "pcol")
    )
    diag_two = inner_two - first_term
    cross_block = -(second_term + product(diag_two, top_one))
    column_one = -(own_live[:, None] * (total_rows(partial_one) + product(column_two, top_one)))
    third_term = lax.psum(contract(own_one, column_one), ("prow", "pcol"))
    diag_one = inner_one - third_term - contract(top_one, cross_block)
    return (column_two, diag_two, column_one, cross_block, diag_one)


def halves(value):
    high = value.astype(BF16)
    return high, (value - high.astype(F32)).astype(BF16)


def dot3(left, right, dims):
    (lh, ll), (rh, rl) = left, right
    dot = lambda a, b: lax.dot_general(a, b, (dims, ((), ())), preferred_element_type=F32)
    return dot(lh, rh) + (dot(lh, rl) + dot(ll, rh))


ROWS_BY_COLUMNS = ((1,), (0,))
ROWS_BY_ROWS = ((0,), (0,))


def keep_rows(block, limit):
    row = lax.broadcasted_iota(jnp.int32, block.shape, 0)
    return jnp.where(row < limit, block, 0.0)


def limits(megabytes):
    return pltpu.CompilerParams(vmem_limit_bytes=megabytes * 2**20)


def cost(flops, moved):
    return pl.CostEstimate(flops=flops, bytes_accessed=moved, transcendentals=0)


def live_rows(at, n, which):
    return at[2 + which]


def kept_rows(at, n, side, which):
    return at[2 + which] * at[2 + n * n * (1 + side) + which]


def masked(block, at, n, which):
    width = block.shape[-1]
    return jnp.concatenate(
        [
            keep_rows(block[side * width : (side + 1) * width], kept_rows(at, n, side, which))
            for side in range(2)
        ],
        axis=1,
    )


def tile_rows(a, col, width):
    return pl.ds(pl.multiple_of((a ^ col) * width, width), width)


def stack_kernel(*refs):
    blocks, out, sems = refs[:-2], refs[-2], refs[-1]
    copies, start = [], 0
    for i, block in enumerate(blocks):
        rows = block.shape[0]
        copies.append(pltpu.make_async_copy(block, out.at[pl.ds(start, rows)], sems.at[i]))
        start += rows
    for copy in copies:
        copy.start()
    for copy in copies:
        copy.wait()


def stack(*blocks):
    rows = sum(block.shape[0] for block in blocks)
    width = blocks[0].shape[1]
    return pl.pallas_call(
        stack_kernel,
        out_shape=jax.ShapeDtypeStruct((rows, width), F32),
        in_specs=[HBM] * len(blocks),
        out_specs=VMEM,
        scratch_shapes=[pltpu.SemaphoreType.DMA((len(blocks),))],
        compiler_params=limits(4),
        cost_estimate=cost(0, 8 * rows * width),
        name="stack_rows",
    )(*blocks)


def left_term(n, a, at, known, two, one):
    row, col = at[0], at[1]
    rows = jnp.concatenate([two, one], axis=0)
    rows = halves(masked(rows, at, n, row * n + (a ^ col)))
    tile = known[tile_rows(a, col, two.shape[0])]
    return dot3(rows, halves(tile), ROWS_BY_ROWS)


def left_first_kernel(n, at, known, here, out):
    blocks = here[...].reshape(4, -1, here.shape[1])
    out[...] = left_term(n, 0, at, known, blocks[0], blocks[1])
    out[...] += left_term(n, 1, at, known, blocks[2], blocks[3])


def left_last_kernel(n, at, known, two, one, core_two, core_one, before, high, low):
    total = before[...] + left_term(n, 2, at, known, two[...], one[...])
    total = total + left_term(n, 3, at, known, core_two[...], core_one[...])
    high[...], low[...] = halves(total)


def call(kernel, name, megabytes, estimate, out_shape, *arrays, scratch=()):
    return pl.pallas_call(
        kernel,
        out_shape=out_shape,
        in_specs=[SMEM] + [VMEM] * (len(arrays) - 1),
        out_specs=jax.tree.map(lambda _: VMEM, out_shape),
        scratch_shapes=scratch,
        compiler_params=limits(megabytes),
        cost_estimate=estimate,
        name=name,
    )(*arrays)


def left_first(n, at, known, here):
    rows, span = known.shape
    shape = jax.ShapeDtypeStruct((2 * rows // n, span), F32)
    kernel = functools.partial(left_first_kernel, n)
    return call(kernel, "left_first", 14, cost(0, 0), shape, at, known, here)


def left_last(n, at, known, there, first):
    half = jax.ShapeDtypeStruct(first.shape, BF16)
    kernel = functools.partial(left_last_kernel, n)
    return call(kernel, "left_last", 14, cost(0, 0), (half, half), at, known, *there, first)


FIRST_ARRIVAL = 1


def arrived_columns(row, m, width):
    return pl.ds(pl.multiple_of(((row >> 1) ^ m) * (2 * width), 2 * width), 2 * width)


def eighth(at, e, h, width):
    part = width // 8
    return pl.multiple_of(((e ^ at[1]) * 2 + (h ^ (at[0] & 1))) * part, part)


def sums_kernel(n, m, at, left_high, left_low, arrived, *refs):
    row, col = at[0], at[1]
    width = arrived.shape[-1]
    high, low = refs[-2:] if len(refs) == 3 else refs[3:5]
    for e in range(2):
        block = row ^ (2 * m + e)
        rows = arrived[2 * e * width : 2 * (e + 1) * width]
        where = pl.ds(pl.multiple_of((block & 1) * width, width), width)
        high[where], low[where] = halves(masked(rows, at, n, col * n + block))
    columns = arrived_columns(row, m, width)
    left = (left_high[:, columns], left_low[:, columns])
    two = (high[:, :width], low[:, :width])
    one = (high[:, width:], low[:, width:])
    first = dot3(left, two, ROWS_BY_COLUMNS)
    second = dot3((left[0][width:], left[1][width:]), one, ROWS_BY_COLUMNS)
    if len(refs) == 3:
        out = refs[0]
        out[: 2 * width] = first
        out[2 * width :] = second
        return
    before, keep, send, total = refs[0], refs[1], refs[2], refs[5]
    total[: 2 * width] = before[: 2 * width] + first
    total[2 * width :] = before[2 * width :] + second
    for e in range(n):
        for h in range(2):
            for s in range(3):
                start = ((e >> 1) * 6 + h * 3 + s) * (width // 8)
                part = total[pl.ds(s * width + eighth(at, e, h, width), width // 8)]
                (send if e & 1 else keep)[start : start + width // 8] = part


def small_sums(n, at, left, arrived):
    width = arrived[0].shape[-1]
    part = jax.ShapeDtypeStruct((2 * width, 2 * width), BF16)
    whole = jax.ShapeDtypeStruct((3 * width, width), F32)
    half = jax.ShapeDtypeStruct((3 * width // 2, width), F32)
    estimate = cost(18 * 2 * width * width * width, 0)
    total, *first = call(
        functools.partial(sums_kernel, n, FIRST_ARRIVAL), "first_sums", 8, estimate,
        (whole, part, part), at, *left, arrived[FIRST_ARRIVAL],
    )
    keep, send, *last = call(
        functools.partial(sums_kernel, n, 1 - FIRST_ARRIVAL), "last_sums", 8, estimate,
        (half, half, part, part), at, *left, arrived[1 - FIRST_ARRIVAL], total,
        scratch=[pltpu.VMEM((3 * width, width), F32)],
    )
    return keep, send, (*first, *last) if FIRST_ARRIVAL == 0 else (*last, *first)


def band_kernel(n, first, at, known, *refs):
    right, out = refs[:4], refs[4]
    row, col = at[0], at[1]
    width = right[0].shape[0] // 2
    for i in range(n // 2):
        tile = tile_rows(first + 2 * i, col, width)
        terms = [
            dot3(
                halves(known[tile, arrived_columns(row, m, width)]),
                (right[2 * m][...], right[2 * m + 1][...]),
                ROWS_BY_COLUMNS,
            )
            for m in range(2)
        ]
        out[i] = terms[0] + terms[1]


def band_product(n, first, at, known, right):
    rows, span = known.shape
    width = rows // n
    return call(
        functools.partial(band_kernel, n, first), "band_product", 14,
        cost(6 * rows * span * width, 2 * rows * span),
        jax.ShapeDtypeStruct((n // 2, width, 2 * width), F32), at, known, *right,
    )


def column_kernel(n, at, keep, got, other, top, two, one):
    width = top.shape[0]
    limit = live_rows(at, n, at[0] * n + at[1])
    total = keep[0] + got[0] + other[...]
    column_two = keep_rows(-total[:, :width], limit)
    two[...] = column_two
    second = total[:, width:] + dot3(halves(column_two), halves(top[...]), ROWS_BY_COLUMNS)
    one[...] = keep_rows(-second, limit)


def columns(n, at, keep, got, other, top):
    shape = jax.ShapeDtypeStruct(top.shape, F32)
    return pl.pallas_call(
        functools.partial(column_kernel, n),
        out_shape=(shape, shape),
        in_specs=[SMEM] + [VMEM] * 4,
        out_specs=(VMEM, VMEM),
        compiler_params=limits(8),
        name="column_rows",
    )(at, keep, got, other, top)


def blocks_kernel(n, at, top, inner_two, inner_one, first, second, diag_two, cross, diag_one, sums):
    width = top.shape[0]
    for e in range(n):
        for h in range(2):
            for s in range(3):
                start = ((e >> 1) * 6 + h * 3 + s) * (width // 8)
                part = (second if e & 1 else first)[start : start + width // 8]
                sums[s, pl.ds(eighth(at, e, h, width), width // 8)] = part
    t = halves(top[...])
    d = inner_two[...] + sums[0]
    diag_two[...] = d
    c = sums[1].T - dot3(halves(d), t, ROWS_BY_COLUMNS)
    cross[...] = c
    diag_one[...] = (
        inner_one[...]
        + sums[2]
        - dot3(halves(sums[1]), t, ROWS_BY_COLUMNS)
        - dot3(t, halves(c), ROWS_BY_ROWS)
    )


def small_blocks(n, at, top, inner_two, inner_one, parts):
    shape = jax.ShapeDtypeStruct(top.shape, F32)
    return pl.pallas_call(
        functools.partial(blocks_kernel, n),
        out_shape=(shape, shape, shape),
        in_specs=[SMEM] + [VMEM] * 5,
        out_specs=(VMEM,) * 3,
        scratch_shapes=[pltpu.VMEM((3,) + top.shape, F32)],
        compiler_params=limits(8),
        name="small_blocks",
    )(at, top, inner_two, inner_one, *parts)


def after(value, *others):
    return lax.optimization_barrier((value, *others))[0]


def square_mesh(
    known, lower_two, lower_one, top_one, inner_two, inner_one, heights, pattern_two, pattern_one
):
    n = lax.axis_size("pcol")
    width = top_one.shape[0]
    place = jnp.stack([lax.axis_index("prow"), lax.axis_index("pcol")]).astype(jnp.int32)
    at = jnp.concatenate([place, heights, pattern_two, pattern_one])

    def along(axis, k, array):
        return lax.ppermute(array, axis, [(i, i ^ k) for i in range(n)])

    core = functools.partial(along, "pcol", 1)
    across = functools.partial(along, "pcol", 2)

    def opposite(rows):
        pairs = [(r * n + c, (r ^ 1) * n + (c ^ 2)) for r in range(n) for c in range(n)]
        return lax.ppermute(rows, ("prow", "pcol"), pairs)

    def direct(k, rows):
        pairs = [(z * n + j, (j ^ k) * n + z) for z in range(n) for j in range(n)]
        return lax.ppermute(rows, ("prow", "pcol"), pairs)

    four = stack(stack(lower_two, lower_one), core(lower_two), core(lower_one))
    gathered = [direct(k, four) for k in range(0, n, 2)]
    first = left_first(n, at, known, four)
    there = [across(lower_two), across(lower_one)]
    there += [core(after(rows, first)) for rows in there]
    left = left_last(n, at, known, there, first)

    keep_sums, send_sums, right = small_sums(n, at, left, gathered)
    mine = keep_sums + core(send_sums)
    send = band_product(n, 1, after(at, mine), known, right)
    keep = band_product(n, 0, after(at, send), known, right)
    own, beyond, beside, corner = jnp.split(mine, 4)
    mine = (own + along("prow", 1, beyond)) + (across(beside) + opposite(corner))
    got = core(after(send, mine))
    other = across(keep[1] + got[1])
    mine = mine + along("prow", 2, mine)
    column_two, column_one = columns(n, at, keep, got, other, top_one)
    both = [mine, along("prow", 1, mine), across(mine), opposite(mine)]
    both = jnp.concatenate([after(both[0], column_one)] + both[1:])
    both = both, core(both)
    diag_two, cross_block, diag_one = small_blocks(n, at, top_one, inner_two, inner_one, both)
    return (column_two, diag_two, column_one, cross_block, diag_one)


def per_device(known, lower_two, lower_one, top_one, *rest):
    square = lax.axis_size("prow") == 4 and lax.axis_size("pcol") == 4
    body = square_mesh if square and lower_two.shape == top_one.shape else any_mesh
    return body(known, lower_two, lower_one, top_one, *rest)


def solution(mesh):
    return jax.shard_map(
        per_device,
        mesh=mesh,
        in_specs=(
            P(("pole", "prow"), "pcol"),
            P(("pole", "prow", "pcol"), None),
            P(("pole", "prow", "pcol"), None),
            P("pole", None),
            P("pole", None),
            P("pole", None),
            P(),
            P(),
            P(),
        ),
        out_specs=(
            P(("pole", "prow", "pcol"), None),
            P("pole", None),
            P(("pole", "prow", "pcol"), None),
            P("pole", None),
            P("pole", None),
        ),
        check_vma=False,
    )
```

```python
import functools

import jax
import jax.numpy as jnp
from jax import lax
from jax.experimental import pallas as pl
from jax.experimental.pallas import tpu as pltpu
from jax.sharding import PartitionSpec as P

F32 = jnp.float32
BF16 = jnp.bfloat16
HBM = pl.BlockSpec(memory_space=pltpu.HBM)
SMEM = pl.BlockSpec(memory_space=pltpu.SMEM)
VMEM = pl.BlockSpec(memory_space=pltpu.VMEM)


def product(left, right):
    return jnp.dot(left, right, precision=lax.Precision.HIGHEST, preferred_element_type=F32)


def contract(left, right):
    return lax.dot_general(
        left, right, (((0,), (0,)), ((), ())), precision=lax.Precision.HIGHEST, preferred_element_type=F32
    )


def spread_2(array, axis, root):
    mine = lax.axis_index(axis) == root
    return lax.psum(jnp.where(mine, array, jnp.zeros_like(array)), axis)


def any_mesh(
    known, lower_two, lower_one, top_one, inner_two, inner_one, heights, pattern_two, pattern_one
):
    width = top_one.shape[0]
    piece = lower_two.shape[0]
    n_col = lax.axis_size("pcol")
    ratio = lax.axis_size("prow") // n_col
    row_index = lax.axis_index("prow")
    col_index = lax.axis_index("pcol")
    live = (jnp.arange(width)[None, :] < heights[:, None]).astype(F32).reshape(-1)
    own_start = (row_index * n_col + col_index) * piece
    own_live = lax.dynamic_slice_in_dim(live, own_start, piece)

    def mask_own(lower, pattern):
        keep = live * jnp.repeat(pattern.astype(F32), width)
        return lower * lax.dynamic_slice_in_dim(keep, own_start, piece)[:, None]

    def spread(own_rows):
        band = lax.all_gather(own_rows, "pcol", axis=0, tiled=True)
        return jnp.concatenate(
            [spread_2(band, "prow", col_index * ratio + offset) for offset in range(ratio)], axis=0
        )

    def total_rows(partial_value):
        return lax.psum_scatter(partial_value, "pcol", scatter_dimension=0, tiled=True)

    own_two = mask_own(lower_two, pattern_two)
    own_one = mask_own(lower_one, pattern_one)
    partial_two = product(known, spread(own_two))
    partial_one = product(known, spread(own_one))
    column_two = -(own_live[:, None] * total_rows(partial_two))
    first_term, second_term = lax.psum(
        (contract(own_two, column_two), contract(column_two, own_one)), ("prow", "pcol")
    )
    diag_two = inner_two - first_term
    cross_block = -(second_term + product(diag_two, top_one))
    column_one = -(own_live[:, None] * (total_rows(partial_one) + product(column_two, top_one)))
    third_term = lax.psum(contract(own_one, column_one), ("prow", "pcol"))
    diag_one = inner_one - third_term - contract(top_one, cross_block)
    return (column_two, diag_two, column_one, cross_block, diag_one)


def halves(value):
    high = value.astype(BF16)
    return high, (value - high.astype(F32)).astype(BF16)


def dot3(left, right, dims):
    (lh, ll), (rh, rl) = left, right
    dot = lambda a, b: lax.dot_general(a, b, (dims, ((), ())), preferred_element_type=F32)
    return dot(lh, rh) + (dot(lh, rl) + dot(ll, rh))


ROWS_BY_COLUMNS = ((1,), (0,))
ROWS_BY_ROWS = ((0,), (0,))


def keep_rows(block, limit):
    row = lax.broadcasted_iota(jnp.int32, block.shape, 0)
    return jnp.where(row < limit, block, 0.0)


def limits(megabytes):
    return pltpu.CompilerParams(vmem_limit_bytes=megabytes * 2**20)


def cost(flops, moved):
    return pl.CostEstimate(flops=flops, bytes_accessed=moved, transcendentals=0)


def live_rows(at, n, which):
    return at[2 + which]


def kept_rows(at, n, side, which):
    return at[2 + which] * at[2 + n * n * (1 + side) + which]


def masked(block, at, n, which):
    width = block.shape[-1]
    return jnp.concatenate(
        [
            keep_rows(block[side * width : (side + 1) * width], kept_rows(at, n, side, which))
            for side in range(2)
        ],
        axis=1,
    )


def tile_rows(a, col, width):
    return pl.ds(pl.multiple_of((a ^ col) * width, width), width)


def stack_kernel(*refs):
    blocks, out, sems = refs[:-2], refs[-2], refs[-1]
    copies, start = [], 0
    for i, block in enumerate(blocks):
        rows = block.shape[0]
        copies.append(pltpu.make_async_copy(block, out.at[pl.ds(start, rows)], sems.at[i]))
        start += rows
    for copy in copies:
        copy.start()
    for copy in copies:
        copy.wait()


def stack(*blocks):
    rows = sum(block.shape[0] for block in blocks)
    width = blocks[0].shape[1]
    return pl.pallas_call(
        stack_kernel,
        out_shape=jax.ShapeDtypeStruct((rows, width), F32),
        in_specs=[HBM] * len(blocks),
        out_specs=VMEM,
        scratch_shapes=[pltpu.SemaphoreType.DMA((len(blocks),))],
        compiler_params=limits(4),
        cost_estimate=cost(0, 8 * rows * width),
        name="stack_rows",
    )(*blocks)


def left_term(n, a, at, known, two, one):
    row, col = at[0], at[1]
    rows = jnp.concatenate([two, one], axis=0)
    rows = halves(masked(rows, at, n, row * n + (a ^ col)))
    tile = known[tile_rows(a, col, two.shape[0])]
    return dot3(rows, halves(tile), ROWS_BY_ROWS)


def left_first_kernel(n, at, known, here, out):
    blocks = here[...].reshape(4, -1, here.shape[1])
    out[...] = left_term(n, 0, at, known, blocks[0], blocks[1])
    out[...] += left_term(n, 1, at, known, blocks[2], blocks[3])


def left_last_kernel(n, at, known, two, one, core_two, core_one, before, high, low):
    total = before[...] + left_term(n, 2, at, known, two[...], one[...])
    total = total + left_term(n, 3, at, known, core_two[...], core_one[...])
    high[...], low[...] = halves(total)


def call(kernel, name, megabytes, estimate, out_shape, *arrays, scratch=()):
    return pl.pallas_call(
        kernel,
        out_shape=out_shape,
        in_specs=[SMEM] + [VMEM] * (len(arrays) - 1),
        out_specs=jax.tree.map(lambda _: VMEM, out_shape),
        scratch_shapes=scratch,
        compiler_params=limits(megabytes),
        cost_estimate=estimate,
        name=name,
    )(*arrays)


def left_first(n, at, known, here):
    rows, span = known.shape
    shape = jax.ShapeDtypeStruct((2 * rows // n, span), F32)
    kernel = functools.partial(left_first_kernel, n)
    return call(kernel, "left_first", 14, cost(0, 0), shape, at, known, here)


def left_last(n, at, known, there, first):
    half = jax.ShapeDtypeStruct(first.shape, BF16)
    kernel = functools.partial(left_last_kernel, n)
    return call(kernel, "left_last", 14, cost(0, 0), (half, half), at, known, *there, first)


FIRST_ARRIVAL = 1


def arrived_columns(row, m, width):
    return pl.ds(pl.multiple_of(((row >> 1) ^ m) * (2 * width), 2 * width), 2 * width)


def eighth(at, e, h, width):
    part = width // 8
    return pl.multiple_of(((e ^ at[1]) * 2 + (h ^ (at[0] & 1))) * part, part)


def sums_kernel(n, m, at, left_high, left_low, arrived, *refs):
    row, col = at[0], at[1]
    width = arrived.shape[-1]
    high, low = refs[-2:] if len(refs) == 3 else refs[3:5]
    for e in range(2):
        block = row ^ (2 * m + e)
        rows = arrived[2 * e * width : 2 * (e + 1) * width]
        where = pl.ds(pl.multiple_of((block & 1) * width, width), width)
        high[where], low[where] = halves(masked(rows, at, n, col * n + block))
    columns = arrived_columns(row, m, width)
    left = (left_high[:, columns], left_low[:, columns])
    two = (high[:, :width], low[:, :width])
    one = (high[:, width:], low[:, width:])
    first = dot3(left, two, ROWS_BY_COLUMNS)
    second = dot3((left[0][width:], left[1][width:]), one, ROWS_BY_COLUMNS)
    if len(refs) == 3:
        out = refs[0]
        out[: 2 * width] = first
        out[2 * width :] = second
        return
    before, keep, send, total = refs[0], refs[1], refs[2], refs[5]
    total[: 2 * width] = before[: 2 * width] + first
    total[2 * width :] = before[2 * width :] + second
    for e in range(n):
        for h in range(2):
            for s in range(3):
                start = ((e >> 1) * 6 + h * 3 + s) * (width // 8)
                part = total[pl.ds(s * width + eighth(at, e, h, width), width // 8)]
                (send if e & 1 else keep)[start : start + width // 8] = part


def small_sums(n, at, left, arrived):
    width = arrived[0].shape[-1]
    part = jax.ShapeDtypeStruct((2 * width, 2 * width), BF16)
    whole = jax.ShapeDtypeStruct((3 * width, width), F32)
    half = jax.ShapeDtypeStruct((3 * width // 2, width), F32)
    estimate = cost(18 * 2 * width * width * width, 0)
    total, *first = call(
        functools.partial(sums_kernel, n, FIRST_ARRIVAL), "first_sums", 8, estimate,
        (whole, part, part), at, *left, arrived[FIRST_ARRIVAL],
    )
    keep, send, *last = call(
        functools.partial(sums_kernel, n, 1 - FIRST_ARRIVAL), "last_sums", 8, estimate,
        (half, half, part, part), at, *left, arrived[1 - FIRST_ARRIVAL], total,
        scratch=[pltpu.VMEM((3 * width, width), F32)],
    )
    return keep, send, (*first, *last) if FIRST_ARRIVAL == 0 else (*last, *first)


def band_kernel(n, first, at, known, *refs):
    right, out = refs[:4], refs[4]
    row, col = at[0], at[1]
    width = right[0].shape[0] // 2
    for i in range(n // 2):
        tile = tile_rows(first + 2 * i, col, width)
        terms = [
            dot3(
                halves(known[tile, arrived_columns(row, m, width)]),
                (right[2 * m][...], right[2 * m + 1][...]),
                ROWS_BY_COLUMNS,
            )
            for m in range(2)
        ]
        out[i] = terms[0] + terms[1]


def band_product(n, first, at, known, right):
    rows, span = known.shape
    width = rows // n
    return call(
        functools.partial(band_kernel, n, first), "band_product", 14,
        cost(6 * rows * span * width, 2 * rows * span),
        jax.ShapeDtypeStruct((n // 2, width, 2 * width), F32), at, known, *right,
    )


def column_kernel(n, at, keep, got, other, top, two, one):
    width = top.shape[0]
    limit = live_rows(at, n, at[0] * n + at[1])
    total = keep[0] + got[0] + other[...]
    column_two = keep_rows(-total[:, :width], limit)
    two[...] = column_two
    second = total[:, width:] + dot3(halves(column_two), halves(top[...]), ROWS_BY_COLUMNS)
    one[...] = keep_rows(-second, limit)


def columns(n, at, keep, got, other, top):
    shape = jax.ShapeDtypeStruct(top.shape, F32)
    return pl.pallas_call(
        functools.partial(column_kernel, n),
        out_shape=(shape, shape),
        in_specs=[SMEM] + [VMEM] * 4,
        out_specs=(VMEM, VMEM),
        compiler_params=limits(8),
        name="column_rows",
    )(at, keep, got, other, top)


def blocks_kernel(n, at, top, inner_two, inner_one, first, second, diag_two, cross, diag_one, sums):
    width = top.shape[0]
    for e in range(n):
        for h in range(2):
            for s in range(3):
                start = ((e >> 1) * 6 + h * 3 + s) * (width // 8)
                part = (second if e & 1 else first)[start : start + width // 8]
                sums[s, pl.ds(eighth(at, e, h, width), width // 8)] = part
    t = halves(top[...])
    d = inner_two[...] + sums[0]
    diag_two[...] = d
    c = sums[1].T - dot3(halves(d), t, ROWS_BY_COLUMNS)
    cross[...] = c
    diag_one[...] = (
        inner_one[...]
        + sums[2]
        - dot3(halves(sums[1]), t, ROWS_BY_COLUMNS)
        - dot3(t, halves(c), ROWS_BY_ROWS)
    )


def small_blocks(n, at, top, inner_two, inner_one, parts):
    shape = jax.ShapeDtypeStruct(top.shape, F32)
    return pl.pallas_call(
        functools.partial(blocks_kernel, n),
        out_shape=(shape, shape, shape),
        in_specs=[SMEM] + [VMEM] * 5,
        out_specs=(VMEM,) * 3,
        scratch_shapes=[pltpu.VMEM((3,) + top.shape, F32)],
        compiler_params=limits(8),
        name="small_blocks",
    )(at, top, inner_two, inner_one, *parts)


def after(value, *others):
    return lax.optimization_barrier((value, *others))[0]


def square_mesh(
    known, lower_two, lower_one, top_one, inner_two, inner_one, heights, pattern_two, pattern_one
):
    n = lax.axis_size("pcol")
    width = top_one.shape[0]
    place = jnp.stack([lax.axis_index("prow"), lax.axis_index("pcol")]).astype(jnp.int32)
    at = jnp.concatenate([place, heights, pattern_two, pattern_one])

    def along(axis, k, array):
        return lax.ppermute(array, axis, [(i, i ^ k) for i in range(n)])

    core = functools.partial(along, "pcol", 1)
    across = functools.partial(along, "pcol", 2)

    def opposite(rows):
        pairs = [(r * n + c, (r ^ 1) * n + (c ^ 2)) for r in range(n) for c in range(n)]
        return lax.ppermute(rows, ("prow", "pcol"), pairs)

    def direct(k, rows):
        pairs = [(z * n + j, (j ^ k) * n + z) for z in range(n) for j in range(n)]
        return lax.ppermute(rows, ("prow", "pcol"), pairs)

    four = stack(stack(lower_two, lower_one), core(lower_two), core(lower_one))
    gathered = [direct(k, four) for k in range(0, n, 2)]
    first = left_first(n, at, known, four)
    there = [across(lower_two), across(lower_one)]
    there += [core(after(rows, first)) for rows in there]
    left = left_last(n, at, known, there, first)

    keep_sums, send_sums, right = small_sums(n, at, left, gathered)
    mine = keep_sums + core(send_sums)
    send = band_product(n, 1, after(at, mine), known, right)
    keep = band_product(n, 0, after(at, send), known, right)
    own, beyond, beside, corner = jnp.split(mine, 4)
    mine = (own + along("prow", 1, beyond)) + (across(beside) + opposite(corner))
    got = core(send)
    other = across(after(keep[1] + got[1], mine))
    mine = mine + along("prow", 2, mine)
    column_two, column_one = columns(n, at, keep, got, other, top_one)
    both = [mine, along("prow", 1, mine), across(mine), opposite(mine)]
    both = jnp.concatenate([after(both[0], other)] + both[1:])
    both = both, core(both)
    diag_two, cross_block, diag_one = small_blocks(n, at, top_one, inner_two, inner_one, both)
    return (column_two, diag_two, column_one, cross_block, diag_one)


def per_device(known, lower_two, lower_one, top_one, *rest):
    square = lax.axis_size("prow") == 4 and lax.axis_size("pcol") == 4
    body = square_mesh if square and lower_two.shape == top_one.shape else any_mesh
    return body(known, lower_two, lower_one, top_one, *rest)


def solution(mesh):
    return jax.shard_map(
        per_device,
        mesh=mesh,
        in_specs=(
            P(("pole", "prow"), "pcol"),
            P(("pole", "prow", "pcol"), None),
            P(("pole", "prow", "pcol"), None),
            P("pole", None),
            P("pole", None),
            P("pole", None),
            P(),
            P(),
            P(),
        ),
        out_specs=(
            P(("pole", "prow", "pcol"), None),
            P("pole", None),
            P(("pole", "prow", "pcol"), None),
            P("pole", None),
            P("pole", None),
        ),
        check_vma=False,
    )
```

```python
import functools

import jax
import jax.numpy as jnp
from jax import lax
from jax.experimental import pallas as pl
from jax.experimental.pallas import tpu as pltpu
from jax.sharding import PartitionSpec as P

F32 = jnp.float32
BF16 = jnp.bfloat16
HBM = pl.BlockSpec(memory_space=pltpu.HBM)
SMEM = pl.BlockSpec(memory_space=pltpu.SMEM)
VMEM = pl.BlockSpec(memory_space=pltpu.VMEM)


def product(left, right):
    return jnp.dot(left, right, precision=lax.Precision.HIGHEST, preferred_element_type=F32)


def contract(left, right):
    return lax.dot_general(
        left, right, (((0,), (0,)), ((), ())), precision=lax.Precision.HIGHEST, preferred_element_type=F32
    )


def spread_2(array, axis, root):
    mine = lax.axis_index(axis) == root
    return lax.psum(jnp.where(mine, array, jnp.zeros_like(array)), axis)


def any_mesh(
    known, lower_two, lower_one, top_one, inner_two, inner_one, heights, pattern_two, pattern_one
):
    width = top_one.shape[0]
    piece = lower_two.shape[0]
    n_col = lax.axis_size("pcol")
    ratio = lax.axis_size("prow") // n_col
    row_index = lax.axis_index("prow")
    col_index = lax.axis_index("pcol")
    live = (jnp.arange(width)[None, :] < heights[:, None]).astype(F32).reshape(-1)
    own_start = (row_index * n_col + col_index) * piece
    own_live = lax.dynamic_slice_in_dim(live, own_start, piece)

    def mask_own(lower, pattern):
        keep = live * jnp.repeat(pattern.astype(F32), width)
        return lower * lax.dynamic_slice_in_dim(keep, own_start, piece)[:, None]

    def spread(own_rows):
        band = lax.all_gather(own_rows, "pcol", axis=0, tiled=True)
        return jnp.concatenate(
            [spread_2(band, "prow", col_index * ratio + offset) for offset in range(ratio)], axis=0
        )

    def total_rows(partial_value):
        return lax.psum_scatter(partial_value, "pcol", scatter_dimension=0, tiled=True)

    own_two = mask_own(lower_two, pattern_two)
    own_one = mask_own(lower_one, pattern_one)
    partial_two = product(known, spread(own_two))
    partial_one = product(known, spread(own_one))
    column_two = -(own_live[:, None] * total_rows(partial_two))
    first_term, second_term = lax.psum(
        (contract(own_two, column_two), contract(column_two, own_one)), ("prow", "pcol")
    )
    diag_two = inner_two - first_term
    cross_block = -(second_term + product(diag_two, top_one))
    column_one = -(own_live[:, None] * (total_rows(partial_one) + product(column_two, top_one)))
    third_term = lax.psum(contract(own_one, column_one), ("prow", "pcol"))
    diag_one = inner_one - third_term - contract(top_one, cross_block)
    return (column_two, diag_two, column_one, cross_block, diag_one)


def halves(value):
    high = value.astype(BF16)
    return high, (value - high.astype(F32)).astype(BF16)


def dot3(left, right, dims):
    (lh, ll), (rh, rl) = left, right
    dot = lambda a, b: lax.dot_general(a, b, (dims, ((), ())), preferred_element_type=F32)
    return dot(lh, rh) + (dot(lh, rl) + dot(ll, rh))


ROWS_BY_COLUMNS = ((1,), (0,))
ROWS_BY_ROWS = ((0,), (0,))


def keep_rows(block, limit):
    row = lax.broadcasted_iota(jnp.int32, block.shape, 0)
    return jnp.where(row < limit, block, 0.0)


def limits(megabytes):
    return pltpu.CompilerParams(vmem_limit_bytes=megabytes * 2**20)


def cost(flops, moved):
    return pl.CostEstimate(flops=flops, bytes_accessed=moved, transcendentals=0)


def live_rows(at, n, which):
    return at[2 + which]


def kept_rows(at, n, side, which):
    return at[2 + which] * at[2 + n * n * (1 + side) + which]


def masked(block, at, n, which):
    width = block.shape[-1]
    return jnp.concatenate(
        [
            keep_rows(block[side * width : (side + 1) * width], kept_rows(at, n, side, which))
            for side in range(2)
        ],
        axis=1,
    )


def tile_rows(a, col, width):
    return pl.ds(pl.multiple_of((a ^ col) * width, width), width)


def stack_kernel(*refs):
    blocks, out, sems = refs[:-2], refs[-2], refs[-1]
    copies, start = [], 0
    for i, block in enumerate(blocks):
        rows = block.shape[0]
        copies.append(pltpu.make_async_copy(block, out.at[pl.ds(start, rows)], sems.at[i]))
        start += rows
    for copy in copies:
        copy.start()
    for copy in copies:
        copy.wait()


def stack(*blocks):
    rows = sum(block.shape[0] for block in blocks)
    width = blocks[0].shape[1]
    return pl.pallas_call(
        stack_kernel,
        out_shape=jax.ShapeDtypeStruct((rows, width), F32),
        in_specs=[HBM] * len(blocks),
        out_specs=VMEM,
        scratch_shapes=[pltpu.SemaphoreType.DMA((len(blocks),))],
        compiler_params=limits(4),
        cost_estimate=cost(0, 8 * rows * width),
        name="stack_rows",
    )(*blocks)


def left_term(n, a, at, known, two, one):
    row, col = at[0], at[1]
    rows = jnp.concatenate([two, one], axis=0)
    rows = halves(masked(rows, at, n, row * n + (a ^ col)))
    tile = known[tile_rows(a, col, two.shape[0])]
    return dot3(rows, halves(tile), ROWS_BY_ROWS)


def left_first_kernel(n, at, known, here, out):
    blocks = here[...].reshape(4, -1, here.shape[1])
    out[...] = left_term(n, 0, at, known, blocks[0], blocks[1])
    out[...] += left_term(n, 1, at, known, blocks[2], blocks[3])


def left_last_kernel(n, at, known, two, one, core_two, core_one, before, high, low):
    total = before[...] + left_term(n, 2, at, known, two[...], one[...])
    total = total + left_term(n, 3, at, known, core_two[...], core_one[...])
    high[...], low[...] = halves(total)


def call(kernel, name, megabytes, estimate, out_shape, *arrays, scratch=()):
    return pl.pallas_call(
        kernel,
        out_shape=out_shape,
        in_specs=[SMEM] + [VMEM] * (len(arrays) - 1),
        out_specs=jax.tree.map(lambda _: VMEM, out_shape),
        scratch_shapes=scratch,
        compiler_params=limits(megabytes),
        cost_estimate=estimate,
        name=name,
    )(*arrays)


def left_first(n, at, known, here):
    rows, span = known.shape
    shape = jax.ShapeDtypeStruct((2 * rows // n, span), F32)
    kernel = functools.partial(left_first_kernel, n)
    return call(kernel, "left_first", 14, cost(0, 0), shape, at, known, here)


def left_last(n, at, known, there, first):
    half = jax.ShapeDtypeStruct(first.shape, BF16)
    kernel = functools.partial(left_last_kernel, n)
    return call(kernel, "left_last", 14, cost(0, 0), (half, half), at, known, *there, first)


FIRST_ARRIVAL = 1


def arrived_columns(row, m, width):
    return pl.ds(pl.multiple_of(((row >> 1) ^ m) * (2 * width), 2 * width), 2 * width)


def eighth(at, e, h, width):
    part = width // 8
    return pl.multiple_of(((e ^ at[1]) * 2 + (h ^ (at[0] & 1))) * part, part)


def sums_kernel(n, m, at, left_high, left_low, arrived, *refs):
    row, col = at[0], at[1]
    width = arrived.shape[-1]
    high, low = refs[-2:] if len(refs) == 3 else refs[3:5]
    for e in range(2):
        block = row ^ (2 * m + e)
        rows = arrived[2 * e * width : 2 * (e + 1) * width]
        where = pl.ds(pl.multiple_of((block & 1) * width, width), width)
        high[where], low[where] = halves(masked(rows, at, n, col * n + block))
    columns = arrived_columns(row, m, width)
    left = (left_high[:, columns], left_low[:, columns])
    two = (high[:, :width], low[:, :width])
    one = (high[:, width:], low[:, width:])
    first = dot3(left, two, ROWS_BY_COLUMNS)
    second = dot3((left[0][width:], left[1][width:]), one, ROWS_BY_COLUMNS)
    if len(refs) == 3:
        out = refs[0]
        out[: 2 * width] = first
        out[2 * width :] = second
        return
    before, keep, send, total = refs[0], refs[1], refs[2], refs[5]
    total[: 2 * width] = before[: 2 * width] + first
    total[2 * width :] = before[2 * width :] + second
    for e in range(n):
        for h in range(2):
            for s in range(3):
                start = ((e >> 1) * 6 + h * 3 + s) * (width // 8)
                part = total[pl.ds(s * width + eighth(at, e, h, width), width // 8)]
                (send if e & 1 else keep)[start : start + width // 8] = part


def first_sums(n, at, left, arrived):
    width = arrived.shape[-1]
    part = jax.ShapeDtypeStruct((2 * width, 2 * width), BF16)
    whole = jax.ShapeDtypeStruct((3 * width, width), F32)
    return call(
        functools.partial(sums_kernel, n, FIRST_ARRIVAL), "first_sums", 8,
        cost(36 * width * width * width, 0), (whole, part, part), at, *left, arrived,
    )


def last_sums(n, at, left, arrived, total):
    width = arrived.shape[-1]
    part = jax.ShapeDtypeStruct((2 * width, 2 * width), BF16)
    half = jax.ShapeDtypeStruct((3 * width // 2, width), F32)
    return call(
        functools.partial(sums_kernel, n, 1 - FIRST_ARRIVAL), "last_sums", 8,
        cost(36 * width * width * width, 0), (half, half, part, part), at, *left, arrived, total,
        scratch=[pltpu.VMEM((3 * width, width), F32)],
    )


def band_kernel(n, first, arrivals, at, known, *refs):
    right, before, out = refs[: 2 * len(arrivals)], refs[2 * len(arrivals) : -1], refs[-1]
    row, col = at[0], at[1]
    width = right[0].shape[0] // 2
    for i in range(n // 2):
        tile = tile_rows(first + 2 * i, col, width)
        terms = [
            dot3(
                halves(known[tile, arrived_columns(row, m, width)]),
                (right[2 * k][...], right[2 * k + 1][...]),
                ROWS_BY_COLUMNS,
            )
            for k, m in enumerate(arrivals)
        ]
        out[i] = functools.reduce(jnp.add, [ref[i] for ref in before] + terms)


def band_product(n, first, arrivals, at, known, right, *before):
    rows, span = known.shape
    width = rows // n
    right = [half for m in arrivals for half in right[2 * m : 2 * m + 2]]
    return call(
        functools.partial(band_kernel, n, first, arrivals), "band_product", 14,
        cost(3 * len(arrivals) * rows * span * width, len(arrivals) * rows * span),
        jax.ShapeDtypeStruct((n // 2, width, 2 * width), F32), at, known, *right, *before,
    )


def column_kernel(n, at, keep, got, other, top, two, one):
    width = top.shape[0]
    limit = live_rows(at, n, at[0] * n + at[1])
    total = keep[0] + got[0] + other[...]
    column_two = keep_rows(-total[:, :width], limit)
    two[...] = column_two
    second = total[:, width:] + dot3(halves(column_two), halves(top[...]), ROWS_BY_COLUMNS)
    one[...] = keep_rows(-second, limit)


def columns(n, at, keep, got, other, top):
    shape = jax.ShapeDtypeStruct(top.shape, F32)
    return pl.pallas_call(
        functools.partial(column_kernel, n),
        out_shape=(shape, shape),
        in_specs=[SMEM] + [VMEM] * 4,
        out_specs=(VMEM, VMEM),
        compiler_params=limits(8),
        name="column_rows",
    )(at, keep, got, other, top)


def blocks_kernel(n, at, top, inner_two, inner_one, first, second, diag_two, cross, diag_one, sums):
    width = top.shape[0]
    for e in range(n):
        for h in range(2):
            for s in range(3):
                start = ((e >> 1) * 6 + h * 3 + s) * (width // 8)
                part = (second if e & 1 else first)[start : start + width // 8]
                sums[s, pl.ds(eighth(at, e, h, width), width // 8)] = part
    t = halves(top[...])
    d = inner_two[...] + sums[0]
    diag_two[...] = d
    c = sums[1].T - dot3(halves(d), t, ROWS_BY_COLUMNS)
    cross[...] = c
    diag_one[...] = (
        inner_one[...]
        + sums[2]
        - dot3(halves(sums[1]), t, ROWS_BY_COLUMNS)
        - dot3(t, halves(c), ROWS_BY_ROWS)
    )


def small_blocks(n, at, top, inner_two, inner_one, parts):
    shape = jax.ShapeDtypeStruct(top.shape, F32)
    return pl.pallas_call(
        functools.partial(blocks_kernel, n),
        out_shape=(shape, shape, shape),
        in_specs=[SMEM] + [VMEM] * 5,
        out_specs=(VMEM,) * 3,
        scratch_shapes=[pltpu.VMEM((3,) + top.shape, F32)],
        compiler_params=limits(8),
        name="small_blocks",
    )(at, top, inner_two, inner_one, *parts)


def after(value, *others):
    return lax.optimization_barrier((value, *others))[0]


def square_mesh(
    known, lower_two, lower_one, top_one, inner_two, inner_one, heights, pattern_two, pattern_one
):
    n = lax.axis_size("pcol")
    width = top_one.shape[0]
    place = jnp.stack([lax.axis_index("prow"), lax.axis_index("pcol")]).astype(jnp.int32)
    at = jnp.concatenate([place, heights, pattern_two, pattern_one])

    def along(axis, k, array):
        return lax.ppermute(array, axis, [(i, i ^ k) for i in range(n)])

    core = functools.partial(along, "pcol", 1)
    across = functools.partial(along, "pcol", 2)

    def opposite(rows):
        pairs = [(r * n + c, (r ^ 1) * n + (c ^ 2)) for r in range(n) for c in range(n)]
        return lax.ppermute(rows, ("prow", "pcol"), pairs)

    def direct(k, rows):
        pairs = [(z * n + j, (j ^ k) * n + z) for z in range(n) for j in range(n)]
        return lax.ppermute(rows, ("prow", "pcol"), pairs)

    four = stack(stack(lower_two, lower_one), core(lower_two), core(lower_one))
    gathered = [direct(k, four) for k in range(0, n, 2)]
    first = left_first(n, at, known, four)
    there = [across(lower_two), across(lower_one)]
    there += [core(after(rows, first)) for rows in there]
    left = left_last(n, at, known, there, first)

    total, *early = first_sums(n, at, left, gathered[FIRST_ARRIVAL])
    early = {FIRST_ARRIVAL: early}
    partial = [
        band_product(n, 1, (FIRST_ARRIVAL,), at, known, (*early[FIRST_ARRIVAL],) * 2)
    ]
    keep_sums, send_sums, *late = last_sums(
        n, after(at, *partial), left, gathered[1 - FIRST_ARRIVAL], total
    )
    right = [half for m in range(2) for half in early.get(m, late)]
    mine = keep_sums + core(send_sums)
    send = band_product(n, 1, (1 - FIRST_ARRIVAL,), after(at, send_sums), known, right, *partial[:1])
    keep = band_product(n, 0, (0, 1), after(at, send), known, right)
    got = core(after(send, mine))
    own, beyond, beside, corner = jnp.split(mine, 4)
    mine = (own + along("prow", 1, beyond)) + (across(beside) + opposite(corner))
    other = across(after(keep[1] + got[1], mine))
    mine = mine + along("prow", 2, mine)
    column_two, column_one = columns(n, at, keep, got, other, top_one)
    both = [mine, along("prow", 1, mine), across(mine), opposite(mine)]
    both = jnp.concatenate([after(both[0], other)] + both[1:])
    both = both, core(both)
    diag_two, cross_block, diag_one = small_blocks(n, at, top_one, inner_two, inner_one, both)
    return (column_two, diag_two, column_one, cross_block, diag_one)


def per_device(known, lower_two, lower_one, top_one, *rest):
    square = lax.axis_size("prow") == 4 and lax.axis_size("pcol") == 4
    body = square_mesh if square and lower_two.shape == top_one.shape else any_mesh
    return body(known, lower_two, lower_one, top_one, *rest)


def solution(mesh):
    return jax.shard_map(
        per_device,
        mesh=mesh,
        in_specs=(
            P(("pole", "prow"), "pcol"),
            P(("pole", "prow", "pcol"), None),
            P(("pole", "prow", "pcol"), None),
            P("pole", None),
            P("pole", None),
            P("pole", None),
            P(),
            P(),
            P(),
        ),
        out_specs=(
            P(("pole", "prow", "pcol"), None),
            P("pole", None),
            P(("pole", "prow", "pcol"), None),
            P("pole", None),
            P("pole", None),
        ),
        check_vma=False,
    )
```

```python
import functools

import jax
import jax.numpy as jnp
from jax import lax
from jax.experimental import pallas as pl
from jax.experimental.pallas import tpu as pltpu
from jax.sharding import PartitionSpec as P

F32 = jnp.float32
BF16 = jnp.bfloat16
HBM = pl.BlockSpec(memory_space=pltpu.HBM)
SMEM = pl.BlockSpec(memory_space=pltpu.SMEM)
VMEM = pl.BlockSpec(memory_space=pltpu.VMEM)


def product(left, right):
    return jnp.dot(left, right, precision=lax.Precision.HIGHEST, preferred_element_type=F32)


def contract(left, right):
    return lax.dot_general(
        left, right, (((0,), (0,)), ((), ())), precision=lax.Precision.HIGHEST, preferred_element_type=F32
    )


def spread_2(array, axis, root):
    mine = lax.axis_index(axis) == root
    return lax.psum(jnp.where(mine, array, jnp.zeros_like(array)), axis)


def any_mesh(
    known, lower_two, lower_one, top_one, inner_two, inner_one, heights, pattern_two, pattern_one
):
    width = top_one.shape[0]
    piece = lower_two.shape[0]
    n_col = lax.axis_size("pcol")
    ratio = lax.axis_size("prow") // n_col
    row_index = lax.axis_index("prow")
    col_index = lax.axis_index("pcol")
    live = (jnp.arange(width)[None, :] < heights[:, None]).astype(F32).reshape(-1)
    own_start = (row_index * n_col + col_index) * piece
    own_live = lax.dynamic_slice_in_dim(live, own_start, piece)

    def mask_own(lower, pattern):
        keep = live * jnp.repeat(pattern.astype(F32), width)
        return lower * lax.dynamic_slice_in_dim(keep, own_start, piece)[:, None]

    def spread(own_rows):
        band = lax.all_gather(own_rows, "pcol", axis=0, tiled=True)
        return jnp.concatenate(
            [spread_2(band, "prow", col_index * ratio + offset) for offset in range(ratio)], axis=0
        )

    def total_rows(partial_value):
        return lax.psum_scatter(partial_value, "pcol", scatter_dimension=0, tiled=True)

    own_two = mask_own(lower_two, pattern_two)
    own_one = mask_own(lower_one, pattern_one)
    partial_two = product(known, spread(own_two))
    partial_one = product(known, spread(own_one))
    column_two = -(own_live[:, None] * total_rows(partial_two))
    first_term, second_term = lax.psum(
        (contract(own_two, column_two), contract(column_two, own_one)), ("prow", "pcol")
    )
    diag_two = inner_two - first_term
    cross_block = -(second_term + product(diag_two, top_one))
    column_one = -(own_live[:, None] * (total_rows(partial_one) + product(column_two, top_one)))
    third_term = lax.psum(contract(own_one, column_one), ("prow", "pcol"))
    diag_one = inner_one - third_term - contract(top_one, cross_block)
    return (column_two, diag_two, column_one, cross_block, diag_one)


def halves(value):
    high = value.astype(BF16)
    return high, (value - high.astype(F32)).astype(BF16)


def dot3(left, right, dims):
    (lh, ll), (rh, rl) = left, right
    dot = lambda a, b: lax.dot_general(a, b, (dims, ((), ())), preferred_element_type=F32)
    return dot(lh, rh) + (dot(lh, rl) + dot(ll, rh))


ROWS_BY_COLUMNS = ((1,), (0,))
ROWS_BY_ROWS = ((0,), (0,))


def keep_rows(block, limit):
    row = lax.broadcasted_iota(jnp.int32, block.shape, 0)
    return jnp.where(row < limit, block, 0.0)


def limits(megabytes):
    return pltpu.CompilerParams(vmem_limit_bytes=megabytes * 2**20)


def cost(flops, moved):
    return pl.CostEstimate(flops=flops, bytes_accessed=moved, transcendentals=0)


def live_rows(at, n, which):
    return at[2 + which]


def kept_rows(at, n, side, which):
    return at[2 + which] * at[2 + n * n * (1 + side) + which]


def masked(block, at, n, which):
    width = block.shape[-1]
    return jnp.concatenate(
        [
            keep_rows(block[side * width : (side + 1) * width], kept_rows(at, n, side, which))
            for side in range(2)
        ],
        axis=1,
    )


def tile_rows(a, col, width):
    return pl.ds(pl.multiple_of((a ^ col) * width, width), width)


def stack_kernel(*refs):
    blocks, out, sems = refs[:-2], refs[-2], refs[-1]
    copies, start = [], 0
    for i, block in enumerate(blocks):
        rows = block.shape[0]
        copies.append(pltpu.make_async_copy(block, out.at[pl.ds(start, rows)], sems.at[i]))
        start += rows
    for copy in copies:
        copy.start()
    for copy in copies:
        copy.wait()


def stack(*blocks):
    rows = sum(block.shape[0] for block in blocks)
    width = blocks[0].shape[1]
    return pl.pallas_call(
        stack_kernel,
        out_shape=jax.ShapeDtypeStruct((rows, width), F32),
        in_specs=[HBM] * len(blocks),
        out_specs=VMEM,
        scratch_shapes=[pltpu.SemaphoreType.DMA((len(blocks),))],
        compiler_params=limits(4),
        cost_estimate=cost(0, 8 * rows * width),
        name="stack_rows",
    )(*blocks)


def left_term(n, a, at, known, two, one):
    row, col = at[0], at[1]
    rows = jnp.concatenate([two, one], axis=0)
    rows = halves(masked(rows, at, n, row * n + (a ^ col)))
    tile = known[tile_rows(a, col, two.shape[0])]
    return dot3(rows, halves(tile), ROWS_BY_ROWS)


def left_first_kernel(n, at, known, here, out):
    blocks = here[...].reshape(4, -1, here.shape[1])
    out[...] = left_term(n, 0, at, known, blocks[0], blocks[1])
    out[...] += left_term(n, 1, at, known, blocks[2], blocks[3])


def left_last_kernel(n, at, known, two, one, core_two, core_one, before, high, low):
    total = before[...] + left_term(n, 2, at, known, two[...], one[...])
    total = total + left_term(n, 3, at, known, core_two[...], core_one[...])
    high[...], low[...] = halves(total)


def call(kernel, name, megabytes, estimate, out_shape, *arrays, scratch=()):
    return pl.pallas_call(
        kernel,
        out_shape=out_shape,
        in_specs=[SMEM] + [VMEM] * (len(arrays) - 1),
        out_specs=jax.tree.map(lambda _: VMEM, out_shape),
        scratch_shapes=scratch,
        compiler_params=limits(megabytes),
        cost_estimate=estimate,
        name=name,
    )(*arrays)


def left_first(n, at, known, here):
    rows, span = known.shape
    shape = jax.ShapeDtypeStruct((2 * rows // n, span), F32)
    kernel = functools.partial(left_first_kernel, n)
    return call(kernel, "left_first", 14, cost(0, 0), shape, at, known, here)


def left_last(n, at, known, there, first):
    half = jax.ShapeDtypeStruct(first.shape, BF16)
    kernel = functools.partial(left_last_kernel, n)
    return call(kernel, "left_last", 14, cost(0, 0), (half, half), at, known, *there, first)


FIRST_ARRIVAL = 1


def arrived_columns(row, m, width):
    return pl.ds(pl.multiple_of(((row >> 1) ^ m) * (2 * width), 2 * width), 2 * width)


def eighth(at, e, h, width):
    part = width // 8
    return pl.multiple_of(((e ^ at[1]) * 2 + (h ^ (at[0] & 1))) * part, part)


def sums_kernel(n, m, at, left_high, left_low, arrived, *refs):
    row, col = at[0], at[1]
    width = arrived.shape[-1]
    high, low = refs[-2:] if len(refs) == 3 else refs[3:5]
    for e in range(2):
        block = row ^ (2 * m + e)
        rows = arrived[2 * e * width : 2 * (e + 1) * width]
        where = pl.ds(pl.multiple_of((block & 1) * width, width), width)
        high[where], low[where] = halves(masked(rows, at, n, col * n + block))
    columns = arrived_columns(row, m, width)
    left = (left_high[:, columns], left_low[:, columns])
    two = (high[:, :width], low[:, :width])
    one = (high[:, width:], low[:, width:])
    first = dot3(left, two, ROWS_BY_COLUMNS)
    second = dot3((left[0][width:], left[1][width:]), one, ROWS_BY_COLUMNS)
    if len(refs) == 3:
        out = refs[0]
        out[: 2 * width] = first
        out[2 * width :] = second
        return
    before, keep, send, total = refs[0], refs[1], refs[2], refs[5]
    total[: 2 * width] = before[: 2 * width] + first
    total[2 * width :] = before[2 * width :] + second
    for e in range(n):
        for h in range(2):
            for s in range(3):
                start = ((e >> 1) * 6 + h * 3 + s) * (width // 8)
                part = total[pl.ds(s * width + eighth(at, e, h, width), width // 8)]
                (send if e & 1 else keep)[start : start + width // 8] = part


def first_sums(n, at, left, arrived):
    width = arrived.shape[-1]
    part = jax.ShapeDtypeStruct((2 * width, 2 * width), BF16)
    whole = jax.ShapeDtypeStruct((3 * width, width), F32)
    return call(
        functools.partial(sums_kernel, n, FIRST_ARRIVAL), "first_sums", 8,
        cost(36 * width * width * width, 0), (whole, part, part), at, *left, arrived,
    )


def last_sums(n, at, left, arrived, total):
    width = arrived.shape[-1]
    part = jax.ShapeDtypeStruct((2 * width, 2 * width), BF16)
    half = jax.ShapeDtypeStruct((3 * width // 2, width), F32)
    return call(
        functools.partial(sums_kernel, n, 1 - FIRST_ARRIVAL), "last_sums", 8,
        cost(36 * width * width * width, 0), (half, half, part, part), at, *left, arrived, total,
        scratch=[pltpu.VMEM((3 * width, width), F32)],
    )


def band_kernel(n, first, arrivals, at, known, *refs):
    right, before, out = refs[: 2 * len(arrivals)], refs[2 * len(arrivals) : -1], refs[-1]
    row, col = at[0], at[1]
    width = right[0].shape[0] // 2
    for i in range(n // 2):
        tile = tile_rows(first + 2 * i, col, width)
        terms = [
            dot3(
                halves(known[tile, arrived_columns(row, m, width)]),
                (right[2 * k][...], right[2 * k + 1][...]),
                ROWS_BY_COLUMNS,
            )
            for k, m in enumerate(arrivals)
        ]
        out[i] = functools.reduce(jnp.add, [ref[i] for ref in before] + terms)


def band_product(n, first, arrivals, at, known, right, *before):
    rows, span = known.shape
    width = rows // n
    right = [half for m in arrivals for half in right[2 * m : 2 * m + 2]]
    return call(
        functools.partial(band_kernel, n, first, arrivals), "band_product", 14,
        cost(3 * len(arrivals) * rows * span * width, len(arrivals) * rows * span),
        jax.ShapeDtypeStruct((n // 2, width, 2 * width), F32), at, known, *right, *before,
    )


def column_kernel(n, at, keep, got, other, top, two, one):
    width = top.shape[0]
    limit = live_rows(at, n, at[0] * n + at[1])
    total = keep[0] + got[0] + other[...]
    column_two = keep_rows(-total[:, :width], limit)
    two[...] = column_two
    second = total[:, width:] + dot3(halves(column_two), halves(top[...]), ROWS_BY_COLUMNS)
    one[...] = keep_rows(-second, limit)


def columns(n, at, keep, got, other, top):
    shape = jax.ShapeDtypeStruct(top.shape, F32)
    return pl.pallas_call(
        functools.partial(column_kernel, n),
        out_shape=(shape, shape),
        in_specs=[SMEM] + [VMEM] * 4,
        out_specs=(VMEM, VMEM),
        compiler_params=limits(8),
        name="column_rows",
    )(at, keep, got, other, top)


def blocks_kernel(n, at, top, inner_two, inner_one, first, second, diag_two, cross, diag_one, sums):
    width = top.shape[0]
    for e in range(n):
        for h in range(2):
            for s in range(3):
                start = ((e >> 1) * 6 + h * 3 + s) * (width // 8)
                part = (second if e & 1 else first)[start : start + width // 8]
                sums[s, pl.ds(eighth(at, e, h, width), width // 8)] = part
    t = halves(top[...])
    d = inner_two[...] + sums[0]
    diag_two[...] = d
    c = sums[1].T - dot3(halves(d), t, ROWS_BY_COLUMNS)
    cross[...] = c
    diag_one[...] = (
        inner_one[...]
        + sums[2]
        - dot3(halves(sums[1]), t, ROWS_BY_COLUMNS)
        - dot3(t, halves(c), ROWS_BY_ROWS)
    )


def small_blocks(n, at, top, inner_two, inner_one, parts):
    shape = jax.ShapeDtypeStruct(top.shape, F32)
    return pl.pallas_call(
        functools.partial(blocks_kernel, n),
        out_shape=(shape, shape, shape),
        in_specs=[SMEM] + [VMEM] * 5,
        out_specs=(VMEM,) * 3,
        scratch_shapes=[pltpu.VMEM((3,) + top.shape, F32)],
        compiler_params=limits(8),
        name="small_blocks",
    )(at, top, inner_two, inner_one, *parts)


def after(value, *others):
    return lax.optimization_barrier((value, *others))[0]


def square_mesh(
    known, lower_two, lower_one, top_one, inner_two, inner_one, heights, pattern_two, pattern_one
):
    n = lax.axis_size("pcol")
    width = top_one.shape[0]
    place = jnp.stack([lax.axis_index("prow"), lax.axis_index("pcol")]).astype(jnp.int32)
    at = jnp.concatenate([place, heights, pattern_two, pattern_one])

    def along(axis, k, array):
        return lax.ppermute(array, axis, [(i, i ^ k) for i in range(n)])

    core = functools.partial(along, "pcol", 1)
    across = functools.partial(along, "pcol", 2)

    def opposite(rows):
        pairs = [(r * n + c, (r ^ 1) * n + (c ^ 2)) for r in range(n) for c in range(n)]
        return lax.ppermute(rows, ("prow", "pcol"), pairs)

    def direct(k, rows):
        pairs = [(z * n + j, (j ^ k) * n + z) for z in range(n) for j in range(n)]
        return lax.ppermute(rows, ("prow", "pcol"), pairs)

    four = stack(stack(lower_two, lower_one), core(lower_two), core(lower_one))
    gathered = [direct(k, four) for k in range(0, n, 2)]
    first = left_first(n, at, known, four)
    there = [across(lower_two), across(lower_one)]
    there += [core(after(rows, first)) for rows in there]
    left = left_last(n, at, known, there, first)

    total, *early = first_sums(n, at, left, gathered[FIRST_ARRIVAL])
    early = {FIRST_ARRIVAL: early}
    partial = [
        band_product(n, 1, (FIRST_ARRIVAL,), at, known, (*early[FIRST_ARRIVAL],) * 2)
    ]
    keep_sums, send_sums, *late = last_sums(
        n, after(at, *partial), left, gathered[1 - FIRST_ARRIVAL], total
    )
    right = [half for m in range(2) for half in early.get(m, late)]
    mine = keep_sums + core(send_sums)
    send = band_product(n, 1, (1 - FIRST_ARRIVAL,), after(at, send_sums), known, right, *partial[:1])
    keep = band_product(n, 0, (0, 1), after(at, send), known, right)
    got = core(after(send, mine))
    own, beyond, beside, corner = jnp.split(mine, 4)
    mine = (own + opposite(corner)) + (across(beside) + along("prow", 1, beyond))
    other = across(after(keep[1] + got[1], mine))
    mine = mine + along("prow", 2, mine)
    column_two, column_one = columns(n, at, keep, got, other, top_one)
    both = [mine, along("prow", 1, mine), across(mine), opposite(mine)]
    both = jnp.concatenate([after(both[0], other)] + both[1:])
    both = both, core(both)
    diag_two, cross_block, diag_one = small_blocks(n, at, top_one, inner_two, inner_one, both)
    return (column_two, diag_two, column_one, cross_block, diag_one)


def per_device(known, lower_two, lower_one, top_one, *rest):
    square = lax.axis_size("prow") == 4 and lax.axis_size("pcol") == 4
    body = square_mesh if square and lower_two.shape == top_one.shape else any_mesh
    return body(known, lower_two, lower_one, top_one, *rest)


def solution(mesh):
    return jax.shard_map(
        per_device,
        mesh=mesh,
        in_specs=(
            P(("pole", "prow"), "pcol"),
            P(("pole", "prow", "pcol"), None),
            P(("pole", "prow", "pcol"), None),
            P("pole", None),
            P("pole", None),
            P("pole", None),
            P(),
            P(),
            P(),
        ),
        out_specs=(
            P(("pole", "prow", "pcol"), None),
            P("pole", None),
            P(("pole", "prow", "pcol"), None),
            P("pole", None),
            P("pole", None),
        ),
        check_vma=False,
    )
```

```python
import functools

import jax
import jax.numpy as jnp
from jax import lax
from jax.experimental import pallas as pl
from jax.experimental.pallas import tpu as pltpu
from jax.sharding import PartitionSpec as P

F32 = jnp.float32
BF16 = jnp.bfloat16
HBM = pl.BlockSpec(memory_space=pltpu.HBM)
VMEM = pl.BlockSpec(memory_space=pltpu.VMEM)


def product(left, right):
    return jnp.dot(left, right, precision=lax.Precision.HIGHEST, preferred_element_type=F32)


def contract(left, right):
    return lax.dot_general(
        left, right, (((0,), (0,)), ((), ())), precision=lax.Precision.HIGHEST, preferred_element_type=F32
    )


def spread_2(array, axis, root):
    mine = lax.axis_index(axis) == root
    return lax.psum(jnp.where(mine, array, jnp.zeros_like(array)), axis)


def any_mesh(
    known, lower_two, lower_one, top_one, inner_two, inner_one, heights, pattern_two, pattern_one
):
    width = top_one.shape[0]
    piece = lower_two.shape[0]
    n_col = lax.axis_size("pcol")
    ratio = lax.axis_size("prow") // n_col
    row_index = lax.axis_index("prow")
    col_index = lax.axis_index("pcol")
    live = (jnp.arange(width)[None, :] < heights[:, None]).astype(F32).reshape(-1)
    own_start = (row_index * n_col + col_index) * piece
    own_live = lax.dynamic_slice_in_dim(live, own_start, piece)

    def mask_own(lower, pattern):
        keep = live * jnp.repeat(pattern.astype(F32), width)
        return lower * lax.dynamic_slice_in_dim(keep, own_start, piece)[:, None]

    def spread(own_rows):
        band = lax.all_gather(own_rows, "pcol", axis=0, tiled=True)
        return jnp.concatenate(
            [spread_2(band, "prow", col_index * ratio + offset) for offset in range(ratio)], axis=0
        )

    def total_rows(partial_value):
        return lax.psum_scatter(partial_value, "pcol", scatter_dimension=0, tiled=True)

    own_two = mask_own(lower_two, pattern_two)
    own_one = mask_own(lower_one, pattern_one)
    partial_two = product(known, spread(own_two))
    partial_one = product(known, spread(own_one))
    column_two = -(own_live[:, None] * total_rows(partial_two))
    first_term, second_term = lax.psum(
        (contract(own_two, column_two), contract(column_two, own_one)), ("prow", "pcol")
    )
    diag_two = inner_two - first_term
    cross_block = -(second_term + product(diag_two, top_one))
    column_one = -(own_live[:, None] * (total_rows(partial_one) + product(column_two, top_one)))
    third_term = lax.psum(contract(own_one, column_one), ("prow", "pcol"))
    diag_one = inner_one - third_term - contract(top_one, cross_block)
    return (column_two, diag_two, column_one, cross_block, diag_one)


def halves(value):
    high = value.astype(BF16)
    return high, (value - high.astype(F32)).astype(BF16)


def dot3(left, right, dims):
    (lh, ll), (rh, rl) = left, right
    dot = lambda a, b: lax.dot_general(a, b, (dims, ((), ())), preferred_element_type=F32)
    return dot(lh, rh) + (dot(lh, rl) + dot(ll, rh))


ROWS_BY_COLUMNS = ((1,), (0,))
ROWS_BY_ROWS = ((0,), (0,))


def keep_rows(block, limit):
    row = lax.broadcasted_iota(jnp.int32, block.shape, 0)
    return jnp.where(row < limit, block, 0.0)


def position():
    return lax.axis_index("prow"), lax.axis_index("pcol")


def limits(megabytes):
    return pltpu.CompilerParams(vmem_limit_bytes=megabytes * 2**20)


def cost(flops, moved):
    return pl.CostEstimate(flops=flops, bytes_accessed=moved, transcendentals=0)


def live_rows(at, n, which):
    return at[pl.ds(which, 1), :]


def kept_rows(at, n, side, which):
    return at[pl.ds(n * n * (1 + side) + which, 1), :]


def masked(block, at, n, which):
    width = block.shape[-1]
    return jnp.concatenate(
        [
            keep_rows(block[side * width : (side + 1) * width], kept_rows(at, n, side, which))
            for side in range(2)
        ],
        axis=1,
    )


def tile_rows(a, col, width):
    return pl.ds(pl.multiple_of((a ^ col) * width, width), width)


def stack_kernel(*refs):
    blocks, out, sems = refs[:-2], refs[-2], refs[-1]
    copies, start = [], 0
    for i, block in enumerate(blocks):
        rows = block.shape[0]
        copies.append(pltpu.make_async_copy(block, out.at[pl.ds(start, rows)], sems.at[i]))
        start += rows
    for copy in copies:
        copy.start()
    for copy in copies:
        copy.wait()


def stack(*blocks):
    rows = sum(block.shape[0] for block in blocks)
    width = blocks[0].shape[1]
    return pl.pallas_call(
        stack_kernel,
        out_shape=jax.ShapeDtypeStruct((rows, width), F32),
        in_specs=[HBM] * len(blocks),
        out_specs=VMEM,
        scratch_shapes=[pltpu.SemaphoreType.DMA((len(blocks),))],
        compiler_params=limits(4),
        cost_estimate=cost(0, 8 * rows * width),
        name="stack_rows",
    )(*blocks)


def left_term(n, a, at, known, two, one):
    row, col = position()
    rows = jnp.concatenate([two, one], axis=0)
    rows = halves(masked(rows, at, n, row * n + (a ^ col)))
    tile = known[tile_rows(a, col, two.shape[0])]
    return dot3(rows, halves(tile), ROWS_BY_ROWS)


def left_first_kernel(n, at, known, here, out):
    blocks = here[...].reshape(4, -1, here.shape[1])
    out[...] = left_term(n, 0, at, known, blocks[0], blocks[1])
    out[...] += left_term(n, 1, at, known, blocks[2], blocks[3])


def left_last_kernel(n, at, known, two, one, core_two, core_one, before, high, low):
    total = before[...] + left_term(n, 2, at, known, two[...], one[...])
    total = total + left_term(n, 3, at, known, core_two[...], core_one[...])
    high[...], low[...] = halves(total)


def call(kernel, name, megabytes, estimate, out_shape, *arrays, scratch=()):
    return pl.pallas_call(
        kernel,
        out_shape=out_shape,
        in_specs=[VMEM] * len(arrays),
        out_specs=jax.tree.map(lambda _: VMEM, out_shape),
        scratch_shapes=scratch,
        compiler_params=limits(megabytes),
        cost_estimate=estimate,
        name=name,
    )(*arrays)


def left_first(n, at, known, here):
    rows, span = known.shape
    shape = jax.ShapeDtypeStruct((2 * rows // n, span), F32)
    kernel = functools.partial(left_first_kernel, n)
    return call(kernel, "left_first", 14, cost(0, 0), shape, at, known, here)


def left_last(n, at, known, there, first):
    half = jax.ShapeDtypeStruct(first.shape, BF16)
    kernel = functools.partial(left_last_kernel, n)
    return call(kernel, "left_last", 14, cost(0, 0), (half, half), at, known, *there, first)


FIRST_ARRIVAL = 1


def arrived_columns(row, m, width):
    return pl.ds(pl.multiple_of(((row >> 1) ^ m) * (2 * width), 2 * width), 2 * width)


def eighth(at, e, h, width):
    part = width // 8
    return pl.multiple_of(((e ^ at[1]) * 2 + (h ^ (at[0] & 1))) * part, part)


def sums_kernel(n, m, at, left_high, left_low, arrived, *refs):
    row, col = position()
    width = arrived.shape[-1]
    high, low = refs[-2:] if len(refs) == 3 else refs[3:5]
    for e in range(2):
        block = row ^ (2 * m + e)
        rows = arrived[2 * e * width : 2 * (e + 1) * width]
        where = pl.ds(pl.multiple_of((block & 1) * width, width), width)
        high[where], low[where] = halves(masked(rows, at, n, col * n + block))
    columns = arrived_columns(row, m, width)
    left = (left_high[:, columns], left_low[:, columns])
    two = (high[:, :width], low[:, :width])
    one = (high[:, width:], low[:, width:])
    first = dot3(left, two, ROWS_BY_COLUMNS)
    second = dot3((left[0][width:], left[1][width:]), one, ROWS_BY_COLUMNS)
    if len(refs) == 3:
        out = refs[0]
        out[: 2 * width] = first
        out[2 * width :] = second
        return
    before, keep, send, total = refs[0], refs[1], refs[2], refs[5]
    total[: 2 * width] = before[: 2 * width] + first
    total[2 * width :] = before[2 * width :] + second
    for e in range(n):
        for h in range(2):
            for s in range(3):
                start = ((e >> 1) * 6 + h * 3 + s) * (width // 8)
                part = total[pl.ds(s * width + eighth(position(), e, h, width), width // 8)]
                (send if e & 1 else keep)[start : start + width // 8] = part


def first_sums(n, at, left, arrived):
    width = arrived.shape[-1]
    part = jax.ShapeDtypeStruct((2 * width, 2 * width), BF16)
    whole = jax.ShapeDtypeStruct((3 * width, width), F32)
    return call(
        functools.partial(sums_kernel, n, FIRST_ARRIVAL), "first_sums", 8,
        cost(36 * width * width * width, 0), (whole, part, part), at, *left, arrived,
    )


def last_sums(n, at, left, arrived, total):
    width = arrived.shape[-1]
    part = jax.ShapeDtypeStruct((2 * width, 2 * width), BF16)
    half = jax.ShapeDtypeStruct((3 * width // 2, width), F32)
    return call(
        functools.partial(sums_kernel, n, 1 - FIRST_ARRIVAL), "last_sums", 8,
        cost(36 * width * width * width, 0), (half, half, part, part), at, *left, arrived, total,
        scratch=[pltpu.VMEM((3 * width, width), F32)],
    )


def band_kernel(n, first, arrivals, known, *refs):
    right, before, out = refs[: 2 * len(arrivals)], refs[2 * len(arrivals) : -1], refs[-1]
    row, col = position()
    width = right[0].shape[0] // 2
    for i in range(n // 2):
        tile = tile_rows(first + 2 * i, col, width)
        terms = [
            dot3(
                halves(known[tile, arrived_columns(row, m, width)]),
                (right[2 * k][...], right[2 * k + 1][...]),
                ROWS_BY_COLUMNS,
            )
            for k, m in enumerate(arrivals)
        ]
        out[i] = functools.reduce(jnp.add, [ref[i] for ref in before] + terms)


def band_product(n, first, arrivals, known, right, *before):
    rows, span = known.shape
    width = rows // n
    right = [half for m in arrivals for half in right[2 * m : 2 * m + 2]]
    return call(
        functools.partial(band_kernel, n, first, arrivals), "band_product", 14,
        cost(3 * len(arrivals) * rows * span * width, len(arrivals) * rows * span),
        jax.ShapeDtypeStruct((n // 2, width, 2 * width), F32), known, *right, *before,
    )


def column_kernel(n, at, keep, got, other, top, two, one):
    width = top.shape[0]
    limit = live_rows(at, n, position()[0] * n + position()[1])
    total = keep[0] + got[0] + other[...]
    column_two = keep_rows(-total[:, :width], limit)
    two[...] = column_two
    second = total[:, width:] + dot3(halves(column_two), halves(top[...]), ROWS_BY_COLUMNS)
    one[...] = keep_rows(-second, limit)


def columns(n, at, keep, got, other, top):
    shape = jax.ShapeDtypeStruct(top.shape, F32)
    return pl.pallas_call(
        functools.partial(column_kernel, n),
        out_shape=(shape, shape),
        in_specs=[VMEM] * 5,
        out_specs=(VMEM, VMEM),
        compiler_params=limits(8),
        name="column_rows",
    )(at, keep, got, other, top)


def blocks_kernel(n, top, inner_two, inner_one, first, second, diag_two, cross, diag_one, sums):
    width = top.shape[0]
    for e in range(n):
        for h in range(2):
            for s in range(3):
                start = ((e >> 1) * 6 + h * 3 + s) * (width // 8)
                part = (second if e & 1 else first)[start : start + width // 8]
                sums[s, pl.ds(eighth(position(), e, h, width), width // 8)] = part
    t = halves(top[...])
    d = inner_two[...] + sums[0]
    diag_two[...] = d
    c = sums[1].T - dot3(halves(d), t, ROWS_BY_COLUMNS)
    cross[...] = c
    diag_one[...] = (
        inner_one[...]
        + sums[2]
        - dot3(halves(sums[1]), t, ROWS_BY_COLUMNS)
        - dot3(t, halves(c), ROWS_BY_ROWS)
    )


def small_blocks(n, top, inner_two, inner_one, parts):
    shape = jax.ShapeDtypeStruct(top.shape, F32)
    return pl.pallas_call(
        functools.partial(blocks_kernel, n),
        out_shape=(shape, shape, shape),
        in_specs=[VMEM] * 5,
        out_specs=(VMEM,) * 3,
        scratch_shapes=[pltpu.VMEM((3,) + top.shape, F32)],
        compiler_params=limits(8),
        name="small_blocks",
    )(top, inner_two, inner_one, *parts)


def after(value, *others):
    return lax.optimization_barrier((value, *others))[0]


def square_mesh(
    known, lower_two, lower_one, top_one, inner_two, inner_one, heights, pattern_two, pattern_one
):
    n = lax.axis_size("pcol")
    width = top_one.shape[0]
    rows = jnp.concatenate([heights, heights * pattern_two, heights * pattern_one])
    at = jnp.broadcast_to(rows[:, None], (rows.shape[0], top_one.shape[1]))

    def along(axis, k, array):
        return lax.ppermute(array, axis, [(i, i ^ k) for i in range(n)])

    core = functools.partial(along, "pcol", 1)
    across = functools.partial(along, "pcol", 2)

    def opposite(rows):
        pairs = [(r * n + c, (r ^ 1) * n + (c ^ 2)) for r in range(n) for c in range(n)]
        return lax.ppermute(rows, ("prow", "pcol"), pairs)

    def direct(k, rows):
        pairs = [(z * n + j, (j ^ k) * n + z) for z in range(n) for j in range(n)]
        return lax.ppermute(rows, ("prow", "pcol"), pairs)

    four = stack(stack(lower_two, lower_one), core(lower_two), core(lower_one))
    gathered = [direct(k, four) for k in range(0, n, 2)]
    first = left_first(n, at, known, four)
    there = [across(lower_two), across(lower_one)]
    there += [core(after(rows, first)) for rows in there]
    left = left_last(n, at, known, there, first)

    total, *early = first_sums(n, at, left, gathered[FIRST_ARRIVAL])
    early = {FIRST_ARRIVAL: early}
    partial = [
        band_product(n, 1, (FIRST_ARRIVAL,), known, (*early[FIRST_ARRIVAL],) * 2)
    ]
    keep_sums, send_sums, *late = last_sums(
        n, after(at, *partial), left, gathered[1 - FIRST_ARRIVAL], total
    )
    right = [half for m in range(2) for half in early.get(m, late)]
    mine = keep_sums + core(send_sums)
    send = band_product(n, 1, (1 - FIRST_ARRIVAL,), after(known, send_sums), right, *partial[:1])
    keep = band_product(n, 0, (0, 1), after(known, send), right)
    got = core(after(send, mine))
    own, beyond, beside, corner = jnp.split(mine, 4)
    mine = (own + opposite(corner)) + (across(beside) + along("prow", 1, beyond))
    other = across(after(keep[1] + got[1], mine))
    mine = mine + along("prow", 2, mine)
    column_two, column_one = columns(n, at, keep, got, other, top_one)
    both = [mine, along("prow", 1, mine), across(mine), opposite(mine)]
    both = jnp.concatenate([after(both[0], other)] + both[1:])
    both = both, core(both)
    diag_two, cross_block, diag_one = small_blocks(n, top_one, inner_two, inner_one, both)
    return (column_two, diag_two, column_one, cross_block, diag_one)


def per_device(known, lower_two, lower_one, top_one, *rest):
    square = lax.axis_size("prow") == 4 and lax.axis_size("pcol") == 4
    body = square_mesh if square and lower_two.shape == top_one.shape else any_mesh
    return body(known, lower_two, lower_one, top_one, *rest)


def solution(mesh):
    return jax.shard_map(
        per_device,
        mesh=mesh,
        in_specs=(
            P(("pole", "prow"), "pcol"),
            P(("pole", "prow", "pcol"), None),
            P(("pole", "prow", "pcol"), None),
            P("pole", None),
            P("pole", None),
            P("pole", None),
            P(),
            P(),
            P(),
        ),
        out_specs=(
            P(("pole", "prow", "pcol"), None),
            P("pole", None),
            P(("pole", "prow", "pcol"), None),
            P("pole", None),
            P("pole", None),
        ),
        check_vma=False,
    )
```

```python
import functools

import jax
import jax.numpy as jnp
from jax import lax
from jax.experimental import pallas as pl
from jax.experimental.pallas import tpu as pltpu
from jax.sharding import PartitionSpec as P

F32 = jnp.float32
BF16 = jnp.bfloat16
HBM = pl.BlockSpec(memory_space=pltpu.HBM)
VMEM = pl.BlockSpec(memory_space=pltpu.VMEM)


def product(left, right):
    return jnp.dot(left, right, precision=lax.Precision.HIGHEST, preferred_element_type=F32)


def contract(left, right):
    return lax.dot_general(
        left, right, (((0,), (0,)), ((), ())), precision=lax.Precision.HIGHEST, preferred_element_type=F32
    )


def spread_2(array, axis, root):
    mine = lax.axis_index(axis) == root
    return lax.psum(jnp.where(mine, array, jnp.zeros_like(array)), axis)


def any_mesh(
    known, lower_two, lower_one, top_one, inner_two, inner_one, heights, pattern_two, pattern_one
):
    width = top_one.shape[0]
    piece = lower_two.shape[0]
    n_col = lax.axis_size("pcol")
    ratio = lax.axis_size("prow") // n_col
    row_index = lax.axis_index("prow")
    col_index = lax.axis_index("pcol")
    live = (jnp.arange(width)[None, :] < heights[:, None]).astype(F32).reshape(-1)
    own_start = (row_index * n_col + col_index) * piece
    own_live = lax.dynamic_slice_in_dim(live, own_start, piece)

    def mask_own(lower, pattern):
        keep = live * jnp.repeat(pattern.astype(F32), width)
        return lower * lax.dynamic_slice_in_dim(keep, own_start, piece)[:, None]

    def spread(own_rows):
        band = lax.all_gather(own_rows, "pcol", axis=0, tiled=True)
        return jnp.concatenate(
            [spread_2(band, "prow", col_index * ratio + offset) for offset in range(ratio)], axis=0
        )

    def total_rows(partial_value):
        return lax.psum_scatter(partial_value, "pcol", scatter_dimension=0, tiled=True)

    own_two = mask_own(lower_two, pattern_two)
    own_one = mask_own(lower_one, pattern_one)
    partial_two = product(known, spread(own_two))
    partial_one = product(known, spread(own_one))
    column_two = -(own_live[:, None] * total_rows(partial_two))
    first_term, second_term = lax.psum(
        (contract(own_two, column_two), contract(column_two, own_one)), ("prow", "pcol")
    )
    diag_two = inner_two - first_term
    cross_block = -(second_term + product(diag_two, top_one))
    column_one = -(own_live[:, None] * (total_rows(partial_one) + product(column_two, top_one)))
    third_term = lax.psum(contract(own_one, column_one), ("prow", "pcol"))
    diag_one = inner_one - third_term - contract(top_one, cross_block)
    return (column_two, diag_two, column_one, cross_block, diag_one)


def halves(value):
    high = value.astype(BF16)
    return high, (value - high.astype(F32)).astype(BF16)


def dot3(left, right, dims):
    (lh, ll), (rh, rl) = left, right
    dot = lambda a, b: lax.dot_general(a, b, (dims, ((), ())), preferred_element_type=F32)
    return dot(lh, rh) + (dot(lh, rl) + dot(ll, rh))


ROWS_BY_COLUMNS = ((1,), (0,))
ROWS_BY_ROWS = ((0,), (0,))


def keep_rows(block, limit):
    row = lax.broadcasted_iota(jnp.int32, block.shape, 0)
    return jnp.where(row < limit, block, 0.0)


def position():
    return lax.axis_index("prow"), lax.axis_index("pcol")


def limits(megabytes):
    return pltpu.CompilerParams(vmem_limit_bytes=megabytes * 2**20)


def cost(flops, moved):
    return pl.CostEstimate(flops=flops, bytes_accessed=moved, transcendentals=0)


def live_rows(at, n, which):
    return at[pl.ds(which, 1), :]


def kept_rows(at, n, side, which):
    return at[pl.ds(n * n * (1 + side) + which, 1), :]


def masked(block, at, n, which):
    width = block.shape[-1]
    return jnp.concatenate(
        [
            keep_rows(block[side * width : (side + 1) * width], kept_rows(at, n, side, which))
            for side in range(2)
        ],
        axis=1,
    )


def tile_rows(a, col, width):
    return pl.ds(pl.multiple_of((a ^ col) * width, width), width)


def stack_kernel(*refs):
    blocks, out, sems = refs[:-2], refs[-2], refs[-1]
    copies, start = [], 0
    for i, block in enumerate(blocks):
        rows = block.shape[0]
        copies.append(pltpu.make_async_copy(block, out.at[pl.ds(start, rows)], sems.at[i]))
        start += rows
    for copy in copies:
        copy.start()
    for copy in copies:
        copy.wait()


def stack(*blocks):
    rows = sum(block.shape[0] for block in blocks)
    width = blocks[0].shape[1]
    return pl.pallas_call(
        stack_kernel,
        out_shape=jax.ShapeDtypeStruct((rows, width), F32),
        in_specs=[HBM] * len(blocks),
        out_specs=VMEM,
        scratch_shapes=[pltpu.SemaphoreType.DMA((len(blocks),))],
        compiler_params=limits(4),
        cost_estimate=cost(0, 8 * rows * width),
        name="stack_rows",
    )(*blocks)


def left_term(n, a, at, known, two, one):
    row, col = position()
    rows = jnp.concatenate([two, one], axis=0)
    rows = halves(masked(rows, at, n, row * n + (a ^ col)))
    tile = known[tile_rows(a, col, two.shape[0])]
    return dot3(rows, halves(tile), ROWS_BY_ROWS)


def left_first_kernel(n, at, known, here, out):
    blocks = here[...].reshape(4, -1, here.shape[1])
    out[...] = left_term(n, 0, at, known, blocks[0], blocks[1])
    out[...] += left_term(n, 1, at, known, blocks[2], blocks[3])


def left_last_kernel(n, at, known, two, one, core_two, core_one, before, high, low):
    total = before[...] + left_term(n, 2, at, known, two[...], one[...])
    total = total + left_term(n, 3, at, known, core_two[...], core_one[...])
    high[...], low[...] = halves(total)


def call(kernel, name, megabytes, estimate, out_shape, *arrays, scratch=()):
    return pl.pallas_call(
        kernel,
        out_shape=out_shape,
        in_specs=[VMEM] * len(arrays),
        out_specs=jax.tree.map(lambda _: VMEM, out_shape),
        scratch_shapes=scratch,
        compiler_params=limits(megabytes),
        cost_estimate=estimate,
        name=name,
    )(*arrays)


def left_first(n, at, known, here):
    rows, span = known.shape
    shape = jax.ShapeDtypeStruct((2 * rows // n, span), F32)
    kernel = functools.partial(left_first_kernel, n)
    return call(kernel, "left_first", 14, cost(0, 0), shape, at, known, here)


def left_last(n, at, known, there, first):
    half = jax.ShapeDtypeStruct(first.shape, BF16)
    kernel = functools.partial(left_last_kernel, n)
    return call(kernel, "left_last", 14, cost(0, 0), (half, half), at, known, *there, first)


FIRST_ARRIVAL = 1


def arrived_columns(row, m, width):
    return pl.ds(pl.multiple_of(((row >> 1) ^ m) * (2 * width), 2 * width), 2 * width)


def eighth(at, e, h, width):
    part = width // 8
    return pl.multiple_of(((e ^ at[1]) * 2 + (h ^ (at[0] & 1))) * part, part)


def sums_kernel(n, m, at, left_high, left_low, arrived, *refs):
    row, col = position()
    width = arrived.shape[-1]
    high, low = refs[-2:] if len(refs) == 3 else refs[3:5]
    for e in range(2):
        block = row ^ (2 * m + e)
        rows = arrived[2 * e * width : 2 * (e + 1) * width]
        where = pl.ds(pl.multiple_of((block & 1) * width, width), width)
        high[where], low[where] = halves(masked(rows, at, n, col * n + block))
    columns = arrived_columns(row, m, width)
    left = (left_high[:, columns], left_low[:, columns])
    two = (high[:, :width], low[:, :width])
    one = (high[:, width:], low[:, width:])
    first = dot3(left, two, ROWS_BY_COLUMNS)
    second = dot3((left[0][width:], left[1][width:]), one, ROWS_BY_COLUMNS)
    if len(refs) == 3:
        out = refs[0]
        out[: 2 * width] = first
        out[2 * width :] = second
        return
    before, keep, send, total = refs[0], refs[1], refs[2], refs[5]
    total[: 2 * width] = before[: 2 * width] + first
    total[2 * width :] = before[2 * width :] + second
    for e in range(n):
        for h in range(2):
            for s in range(3):
                start = ((e >> 1) * 6 + h * 3 + s) * (width // 8)
                part = total[pl.ds(s * width + eighth(position(), e, h, width), width // 8)]
                (send if e & 1 else keep)[start : start + width // 8] = part


def first_sums(n, at, left, arrived):
    width = arrived.shape[-1]
    part = jax.ShapeDtypeStruct((2 * width, 2 * width), BF16)
    whole = jax.ShapeDtypeStruct((3 * width, width), F32)
    return call(
        functools.partial(sums_kernel, n, FIRST_ARRIVAL), "first_sums", 8,
        cost(36 * width * width * width, 0), (whole, part, part), at, *left, arrived,
    )


def last_sums(n, at, left, arrived, total):
    width = arrived.shape[-1]
    part = jax.ShapeDtypeStruct((2 * width, 2 * width), BF16)
    half = jax.ShapeDtypeStruct((3 * width // 2, width), F32)
    return call(
        functools.partial(sums_kernel, n, 1 - FIRST_ARRIVAL), "last_sums", 8,
        cost(36 * width * width * width, 0), (half, half, part, part), at, *left, arrived, total,
        scratch=[pltpu.VMEM((3 * width, width), F32)],
    )


def band_kernel(n, first, arrivals, known, *refs):
    right, before, out = refs[: 2 * len(arrivals)], refs[2 * len(arrivals) : -1], refs[-1]
    row, col = position()
    width = right[0].shape[0] // 2
    for i in range(n // 2):
        tile = tile_rows(first + 2 * i, col, width)
        terms = [
            dot3(
                halves(known[tile, arrived_columns(row, m, width)]),
                (right[2 * k][...], right[2 * k + 1][...]),
                ROWS_BY_COLUMNS,
            )
            for k, m in enumerate(arrivals)
        ]
        out[i] = functools.reduce(jnp.add, [ref[i] for ref in before] + terms)


def band_product(n, first, arrivals, known, right, *before):
    rows, span = known.shape
    width = rows // n
    right = [half for m in arrivals for half in right[2 * m : 2 * m + 2]]
    return call(
        functools.partial(band_kernel, n, first, arrivals), "band_product", 14,
        cost(3 * len(arrivals) * rows * span * width, len(arrivals) * rows * span),
        jax.ShapeDtypeStruct((n // 2, width, 2 * width), F32), known, *right, *before,
    )


def column_kernel(n, at, keep, got, other, top, two, one):
    width = top.shape[0]
    limit = live_rows(at, n, position()[0] * n + position()[1])
    total = keep[0] + got[0] + other[...]
    column_two = keep_rows(-total[:, :width], limit)
    two[...] = column_two
    second = total[:, width:] + dot3(halves(column_two), halves(top[...]), ROWS_BY_COLUMNS)
    one[...] = keep_rows(-second, limit)


def columns(n, at, keep, got, other, top):
    shape = jax.ShapeDtypeStruct(top.shape, F32)
    return pl.pallas_call(
        functools.partial(column_kernel, n),
        out_shape=(shape, shape),
        in_specs=[VMEM] * 5,
        out_specs=(VMEM, VMEM),
        compiler_params=limits(8),
        name="column_rows",
    )(at, keep, got, other, top)


def blocks_kernel(n, top, inner_two, inner_one, first, second, *refs):
    outs, (sums, blocks, sems) = refs[:3], refs[3:]
    copies = [pltpu.make_async_copy(blocks.at[i], outs[i], sems.at[i]) for i in range(3)]
    width = top.shape[0]
    for e in range(n):
        for h in range(2):
            for s in range(3):
                start = ((e >> 1) * 6 + h * 3 + s) * (width // 8)
                part = (second if e & 1 else first)[start : start + width // 8]
                sums[s, pl.ds(eighth(position(), e, h, width), width // 8)] = part
    t = halves(top[...])
    d = inner_two[...] + sums[0]
    blocks[0] = d
    copies[0].start()
    c = sums[1].T - dot3(halves(d), t, ROWS_BY_COLUMNS)
    blocks[1] = c
    copies[1].start()
    blocks[2] = (
        inner_one[...]
        + sums[2]
        - dot3(halves(sums[1]), t, ROWS_BY_COLUMNS)
        - dot3(t, halves(c), ROWS_BY_ROWS)
    )
    copies[2].start()
    for copy in copies:
        copy.wait()


def small_blocks(n, top, inner_two, inner_one, parts):
    shape = jax.ShapeDtypeStruct(top.shape, F32)
    return pl.pallas_call(
        functools.partial(blocks_kernel, n),
        out_shape=(shape, shape, shape),
        in_specs=[VMEM] * 5,
        out_specs=(HBM,) * 3,
        scratch_shapes=[
            pltpu.VMEM((3,) + top.shape, F32),
            pltpu.VMEM((3,) + top.shape, F32),
            pltpu.SemaphoreType.DMA((3,)),
        ],
        compiler_params=limits(8),
        name="small_blocks",
    )(top, inner_two, inner_one, *parts)


def after(value, *others):
    return lax.optimization_barrier((value, *others))[0]


def square_mesh(
    known, lower_two, lower_one, top_one, inner_two, inner_one, heights, pattern_two, pattern_one
):
    n = lax.axis_size("pcol")
    width = top_one.shape[0]
    rows = jnp.concatenate([heights, heights * pattern_two, heights * pattern_one])
    at = jnp.broadcast_to(rows[:, None], (rows.shape[0], top_one.shape[1]))

    def along(axis, k, array):
        return lax.ppermute(array, axis, [(i, i ^ k) for i in range(n)])

    core = functools.partial(along, "pcol", 1)
    across = functools.partial(along, "pcol", 2)

    def opposite(rows):
        pairs = [(r * n + c, (r ^ 1) * n + (c ^ 2)) for r in range(n) for c in range(n)]
        return lax.ppermute(rows, ("prow", "pcol"), pairs)

    def direct(k, rows):
        pairs = [(z * n + j, (j ^ k) * n + z) for z in range(n) for j in range(n)]
        return lax.ppermute(rows, ("prow", "pcol"), pairs)

    four = stack(stack(lower_two, lower_one), core(lower_two), core(lower_one))
    gathered = [direct(k, four) for k in range(0, n, 2)]
    first = left_first(n, at, known, four)
    there = [across(lower_two), across(lower_one)]
    there += [core(after(rows, first)) for rows in there]
    left = left_last(n, at, known, there, first)

    total, *early = first_sums(n, at, left, gathered[FIRST_ARRIVAL])
    early = {FIRST_ARRIVAL: early}
    partial = [
        band_product(n, 1, (FIRST_ARRIVAL,), known, (*early[FIRST_ARRIVAL],) * 2)
    ]
    keep_sums, send_sums, *late = last_sums(
        n, after(at, *partial), left, gathered[1 - FIRST_ARRIVAL], total
    )
    right = [half for m in range(2) for half in early.get(m, late)]
    mine = keep_sums + core(send_sums)
    send = band_product(n, 1, (1 - FIRST_ARRIVAL,), after(known, send_sums), right, *partial[:1])
    keep = band_product(n, 0, (0, 1), after(known, send), right)
    got = core(after(send, mine))
    own, beyond, beside, corner = jnp.split(mine, 4)
    mine = (own + opposite(corner)) + (across(beside) + along("prow", 1, beyond))
    other = across(after(keep[1] + got[1], mine))
    mine = mine + along("prow", 2, mine)
    column_two, column_one = columns(n, at, keep, got, other, top_one)
    both = [mine, along("prow", 1, mine), across(mine), opposite(mine)]
    both = jnp.concatenate([after(both[0], other)] + both[1:])
    both = both, core(both)
    diag_two, cross_block, diag_one = small_blocks(n, top_one, inner_two, inner_one, both)
    return (column_two, diag_two, column_one, cross_block, diag_one)


def per_device(known, lower_two, lower_one, top_one, *rest):
    square = lax.axis_size("prow") == 4 and lax.axis_size("pcol") == 4
    body = square_mesh if square and lower_two.shape == top_one.shape else any_mesh
    return body(known, lower_two, lower_one, top_one, *rest)


def solution(mesh):
    return jax.shard_map(
        per_device,
        mesh=mesh,
        in_specs=(
            P(("pole", "prow"), "pcol"),
            P(("pole", "prow", "pcol"), None),
            P(("pole", "prow", "pcol"), None),
            P("pole", None),
            P("pole", None),
            P("pole", None),
            P(),
            P(),
            P(),
        ),
        out_specs=(
            P(("pole", "prow", "pcol"), None),
            P("pole", None),
            P(("pole", "prow", "pcol"), None),
            P("pole", None),
            P("pole", None),
        ),
        check_vma=False,
    )
```
